128 devices in a mesh: gx: 64 (over z, x_lo, y, core), col: 2 (over x_hi).
Axes of the slice: x: 4 (x_hi: 2, x_lo: 2; x = x_hi * 2 + x_lo), y: 4, z: 4, core: 2. Of those that a mesh axis runs over, the one named last changes fastest.
Arguments:
- state_field: bfloat16 [1024, 64, 8192], P('gx', 'col'), may hold values from -6 to 6
- spectral_weight: bfloat16 [2, 64, 64, 8192], P(None, None, 'col', 'gx'), may hold values from -0.75 to 0.75
- local_weight: float32 [64], P('col'), may hold values from 0.5 to 1.5
- channel_bias: float32 [64], P('col'), may hold values from -3 to 3
Outputs:
- layer_out: bfloat16 [1024, 64, 8192], P('gx', 'col')
The draws below stay inside these ranges and needn't reach their ends.
All inputs are finite; a program needn't handle non-finite values.
Results may differ from the reference program's by a relative error of at most 0.0085.
Values may be sent and summed in bfloat16 or wider, within the bound.
A program may use at most 128 MiB of HBM per device.

```python
import math
from functools import partial
import jax
import jax.numpy as jnp
from jax import lax

XDEV = 16
CH = 64
YCELLS = 128
TSTEPS = 64
KX = 32
KY = 32
KT = 8
XCELLS = 1024
MODES = 8192
N_GX = 64


def block_scale(stream_key, extent, split, least, high):
    factor_of, own = 1.0, jax.random.fold_in(stream_key, 6)
    for axis_at, parts in split:
        heights = jnp.exp(jax.random.uniform(jax.random.fold_in(own, axis_at), (parts,), jnp.float32, least / len(split), high / len(split)))
        factor_of = factor_of * jnp.repeat(heights, extent[axis_at] // parts).reshape([-1 if axis == axis_at else 1 for axis in range(len(extent))])
    return factor_of


def centred(stream_key, extent, scale, most, split=(), kind=jnp.bfloat16):
    drawn = jax.random.normal(stream_key, extent, jnp.float32) * scale
    if len(split) > 0:
        drawn = block_scale(stream_key, extent, split, -0.22, 0.18) * drawn
    return jnp.clip(drawn, min=-most, max=most).astype(kind)


def setup_inputs(seed: int = 0) -> dict:
    key_of = jax.random.split(jax.random.key(seed), 5)
    return {
        "state_field": centred(key_of[0], (XCELLS, CH, YCELLS * TSTEPS), 1.0, 6.0, ((0, 64), (1, 2))),
        "spectral_weight": centred(key_of[1], (2, CH, CH, MODES), CH ** -0.5, 0.75, ((2, 2), (3, 64))),
        "local_weight": jnp.clip(0.5 + 1.0 * jax.random.uniform(key_of[2], (CH,), jnp.float32) ** block_scale(key_of[2], (CH,), ((0, 2),), -0.2, 0.2), 0.5, 1.5),
        "channel_bias": centred(key_of[3], (CH,), 0.5, 3.0, ((0, 2),), jnp.float32),
    }


def frequencies(number_modes):
    positions = jnp.arange(number_modes, dtype=jnp.int32)
    return jnp.where(positions < number_modes // 2, positions, positions - number_modes)

def yt_tables():
    y_index = jnp.arange(YCELLS, dtype=jnp.int32)
    t_index = jnp.arange(TSTEPS, dtype=jnp.int32)
    y_freq = frequencies(KY)
    t_freq = jnp.arange(KT, dtype=jnp.int32)
    phases = (y_index[:, None, None, None] * y_freq[None, None, :, None] * TSTEPS + t_index[None, :, None, None] * t_freq[None, None, None, :] * YCELLS) % (YCELLS * TSTEPS)
    phases = phases.reshape(YCELLS * TSTEPS, KY * KT)
    angles = phases.astype(jnp.float32) * (2.0 * math.pi / (YCELLS * TSTEPS))
    cosine_table = jnp.cos(angles)
    sine_table = jnp.sin(angles)
    time_weights = jnp.tile(jnp.where(t_freq == 0, 1.0, 2.0).astype(jnp.float32), KY)
    forward_table = jnp.concatenate([cosine_table, -sine_table], axis=1).astype(jnp.bfloat16)
    inverse_table = jnp.concatenate([time_weights * cosine_table, -time_weights * sine_table], axis=1).T.astype(jnp.bfloat16)
    return (forward_table, inverse_table)

def x_tables(positions, period):
    phases = positions[:, None] * frequencies(KX)[None, :] % period
    angles = phases.astype(jnp.float32) * (2.0 * math.pi / period)
    return (jnp.cos(angles), jnp.sin(angles))

def forward_x(spectra, cosine_table, sine_table):
    einsum_high = partial(jnp.einsum, precision=lax.Precision.HIGHEST)
    real_part = spectra[:, :, 0]
    imag_part = spectra[:, :, 1]
    out_real = einsum_high('xck,xm->ckm', real_part, cosine_table) + einsum_high('xck,xm->ckm', imag_part, sine_table)
    out_imag = einsum_high('xck,xm->ckm', imag_part, cosine_table) - einsum_high('xck,xm->ckm', real_part, sine_table)
    return jnp.stack([out_real, out_imag], axis=1)

def inverse_x(mode_values, cosine_table, sine_table):
    einsum_high = partial(jnp.einsum, precision=lax.Precision.HIGHEST)
    real_part = mode_values[:, 0]
    imag_part = mode_values[:, 1]
    out_real = einsum_high('ckm,xm->xck', real_part, cosine_table) - einsum_high('ckm,xm->xck', imag_part, sine_table)
    out_imag = einsum_high('ckm,xm->xck', real_part, sine_table) + einsum_high('ckm,xm->xck', imag_part, cosine_table)
    return jnp.stack([out_real, out_imag], axis=2)

def mix_modes(mode_values, weight):
    einsum_high = partial(jnp.einsum, precision=lax.Precision.HIGHEST)
    mode_real = mode_values[:, 0].astype(jnp.float32)
    mode_imag = mode_values[:, 1].astype(jnp.float32)
    weight_real = weight[0].astype(jnp.float32)
    weight_imag = weight[1].astype(jnp.float32)
    out_real = einsum_high('iom,im->om', weight_real, mode_real) - einsum_high('iom,im->om', weight_imag, mode_imag)
    out_imag = einsum_high('iom,im->om', weight_real, mode_imag) + einsum_high('iom,im->om', weight_imag, mode_real)
    return jnp.stack([out_real, out_imag], axis=1)

def reference(state_field, spectral_weight, local_weight, channel_bias):
    forward_table, inverse_table = yt_tables()
    spectra = jnp.dot(state_field.reshape(XCELLS * CH, YCELLS * TSTEPS), forward_table, preferred_element_type=jnp.float32).reshape(XCELLS, CH, 2, KY * KT)
    cosine_table, sine_table = x_tables(jnp.arange(XCELLS, dtype=jnp.int32), XCELLS)
    forward_scale = 1.0 / math.sqrt(XCELLS * YCELLS * TSTEPS)
    mode_values = (forward_x(spectra, cosine_table, sine_table) * forward_scale).reshape(CH, 2, MODES)
    mode_values = mode_values.astype(jnp.bfloat16)
    mixed_all = mix_modes(mode_values, spectral_weight).astype(jnp.bfloat16)
    mixed_all = mixed_all.astype(jnp.float32).reshape(CH, 2, KY * KT, KX)
    slab_values = inverse_x(mixed_all, cosine_table, sine_table).astype(jnp.bfloat16)
    inverse_scale = 1.0 / math.sqrt(MODES)
    blocks_in = slab_values.reshape(N_GX, XDEV * CH, 2 * KY * KT)
    fields_in = state_field.reshape(N_GX, XDEV, CH, YCELLS * TSTEPS)

    def one_block(pair):
        block_modes, block_field = pair
        spectral_out = jnp.dot(block_modes, inverse_table, preferred_element_type=jnp.float32) * inverse_scale
        spectral_out = spectral_out.reshape(XDEV, CH, YCELLS * TSTEPS)
        summed = spectral_out + local_weight[None, :, None] * block_field.astype(jnp.float32) + channel_bias[None, :, None]
        return jax.nn.gelu(summed, approximate=True).astype(jnp.bfloat16)
    layer_out = lax.map(one_block, (blocks_in, fields_in))
    return layer_out.reshape(XCELLS, CH, YCELLS * TSTEPS)
```

```python
import math

import jax
import jax.numpy as jnp
import ml_dtypes
import numpy as np
from jax import lax
from jax.experimental import pallas as pl
from jax.experimental.pallas import tpu as pltpu
from jax.sharding import PartitionSpec as P

MESH = pl.DeviceIdType.MESH
BF16 = jnp.bfloat16
F32 = jnp.float32

XCELLS = 1024
YCELLS = 128
TSTEPS = 64
KX = 32
KY = 32
KT = 8
PLANE = YCELLS * TSTEPS
FOLD = PLANE // 2
SLABS = 64
XDEV = 16
GROUP = 32
ROWS = XDEV * GROUP
HALF = ROWS // 2
PIECES = 4
PIECE = FOLD // PIECES
STEP = 512

NT = (((1,), (1,)), ((), ()))
TN = (((0,), (0,)), ((), ()))


def freq(index, number):
    return np.where(index < number // 2, index, index - number)


def plane_table():
    p, z, yh, xlo, half, r, kt4 = np.meshgrid(
        *[np.arange(n) for n in (2, 4, 2, 2, 2, 2, 4)], indexing="ij"
    )
    ky = freq((z * 8 + xlo * 4 + yh * 2 + p).reshape(-1), KY)
    kt = (half * 4 + kt4).reshape(-1)
    r = r.reshape(-1)
    cells = np.arange(FOLD)
    y, t = cells // TSTEPS, cells % TSTEPS
    phase = (ky[:, None] * y[None] * TSTEPS + kt[:, None] * t[None] * YCELLS) % PLANE
    angle = phase * (2.0 * math.pi / PLANE)
    table = np.where(r[:, None] == 0, np.cos(angle), -np.sin(angle))
    return table.astype(ml_dtypes.bfloat16)


def forward_x_table():
    kx = freq(np.arange(KX), KX)
    slot = np.arange(16)
    p, z, yh = slot // 8, (slot // 2) % 4, slot % 2
    angle = 2.0 * math.pi * ((kx[:, None] * (8 * z + yh * 2 + p)[None]) % 32) / 32
    cosine, sine = np.cos(angle), np.sin(angle)
    table = np.zeros((4, 2, 4, KX, 16, 4, 2, 4))
    for block in range(4):
        for k in range(4):
            table[block, 0, k, :, :, block, 0, k] = cosine
            table[block, 0, k, :, :, block, 1, k] = sine
            table[block, 1, k, :, :, block, 1, k] = cosine
            table[block, 1, k, :, :, block, 0, k] = -sine
    return table.reshape(1024, 512).astype(ml_dtypes.bfloat16)


def forward_twiddle():
    kx = freq(np.arange(KX), KX)
    scale = 1.0 / math.sqrt(XCELLS * PLANE)
    place = np.arange(4)
    offset = (place // 2) * 128 + (place % 2) * 16
    lanes = np.arange(ROWS) // GROUP
    angle = 2.0 * math.pi * ((kx[None, :, None] * (offset[:, None, None] + lanes)) % XCELLS) / XCELLS
    return (np.stack([np.cos(angle), np.sin(angle)], axis=1) * scale).astype(np.float32)


def inverse_x_table():
    kx = freq(np.arange(KX), KX)
    angle = 2.0 * math.pi * ((kx[None] * (8 * np.arange(128))[:, None]) % XCELLS) / XCELLS
    cosine, sine = np.cos(angle), np.sin(angle)
    table = np.zeros((128, 2, 4, 2, 4, KX))
    for k in range(4):
        table[:, 0, k, 0, k] = cosine
        table[:, 0, k, 1, k] = -sine
        table[:, 1, k, 0, k] = sine
        table[:, 1, k, 1, k] = cosine
    return table.reshape(1024, 256).astype(ml_dtypes.bfloat16)


def inverse_twiddle():
    kx = np.tile(freq(np.arange(KX), KX), 4)
    kt4 = np.repeat(np.arange(4), KX)
    lanes = np.arange(HALF) // GROUP
    angle = 2.0 * math.pi * ((kx[:, None] * lanes[None]) % XCELLS) / XCELLS
    parts = np.stack([np.cos(angle), np.sin(angle)])
    weight = np.stack([np.where(kt4 + 4 * half == 0, 1.0, 2.0) for half in range(2)])
    scale = 0.5 / math.sqrt(PLANE)
    return (parts[None] * weight[:, None, :, None] * scale).astype(np.float32)


def place_of(g):
    return g // 16, (g // 8) % 2, (g // 2) % 4, g % 2


def exchange_kernel(
    state, weight, table, fxt, ftw, ixt, itw, out,
    xbuf, tbuf, wbuf, fxt_v, ftw_v, ixt_v, itw_v,
    send1, recv1, partial, send2, recv2, modes, send3, recv3,
    tsem, xsem, csem, ssem, rsem,
):
    g = lax.axis_index("gx")
    col = lax.axis_index("col")
    z, xlo, y, core = place_of(g)

    def zy_partner(k):
        z2, y2 = (z + k // 4) % 4, (y + k % 4) % 4
        return z2 * 16 + xlo * 8 + y2 * 2 + core, (y2 % 2) * 8 + z2 * 2 + y2 // 2

    def near_partner(k):
        xlo2, core2, col2 = (xlo + (k // 2) % 2) % 2, (core + k % 2) % 2, (col + k // 4) % 2
        return z * 16 + xlo2 * 8 + y * 2 + core2, col2, xlo2 * 2 + core2

    loads = []
    for k in range(PIECES):
        cols = pl.ds(k * PIECE, PIECE)
        loads.append(pltpu.make_async_copy(table.at[:, cols], tbuf.at[:, cols], tsem.at[k]))
        loads[-1].start()
        for s in range(2):
            at = pl.ds(s * FOLD + k * PIECE, PIECE)
            pltpu.make_async_copy(
                state.at[pl.ds(0, HALF), at], xbuf.at[pl.ds(0, HALF), at], xsem.at[k * 2 + s]
            ).start()
    for k in range(PIECES):
        for s in range(2):
            at = pl.ds(s * FOLD + k * PIECE, PIECE)
            pltpu.make_async_copy(
                state.at[pl.ds(HALF, HALF), at],
                xbuf.at[pl.ds(HALF, HALF), at],
                xsem.at[2 * PIECES + k * 2 + s],
            ).start()
    constants = [
        pltpu.make_async_copy(fxt, fxt_v, csem.at[0]),
        pltpu.make_async_copy(ftw.at[xlo * 2 + core], ftw_v, csem.at[1]),
        pltpu.make_async_copy(weight, wbuf, csem.at[2]),
        pltpu.make_async_copy(itw.at[core], itw_v, csem.at[3]),
        pltpu.make_async_copy(ixt, ixt_v, csem.at[4]),
    ]
    for copy in constants:
        copy.start()

    barrier = pltpu.get_barrier_semaphore()

    @pl.loop(1, 64)
    def _(k):
        pl.semaphore_signal(barrier, inc=1, device_id=((g + k) % 64, col), device_id_type=MESH)

    @pl.loop(4, 8)
    def _(k):
        to, col2, _slot = near_partner(k)
        pl.semaphore_signal(barrier, inc=1, device_id=(to, col2), device_id_type=MESH)

    mine1 = (y % 2) * 8 + z * 2 + y // 2
    for h in range(2):
        rows = pl.ds(h * HALF, HALF)
        even = jnp.zeros((256, HALF), F32)
        odd = jnp.zeros((256, HALF), F32)
        for k in range(PIECES):
            lo = pl.ds(k * PIECE, PIECE)
            hi = pl.ds(FOLD + k * PIECE, PIECE)
            if h == 0:
                loads[k].wait()
            for s, at in ((0, lo), (1, hi)):
                pltpu.make_async_copy(
                    state.at[rows, at], xbuf.at[rows, at], xsem.at[h * 2 * PIECES + k * 2 + s]
                ).wait()
            x0, x1 = xbuf[rows, lo], xbuf[rows, hi]
            even += lax.dot_general(tbuf[0:256, lo], x0 + x1, NT, preferred_element_type=F32)
            odd += lax.dot_general(tbuf[256:512, lo], x0 - x1, NT, preferred_element_type=F32)
        send1[h, 0:8] = even.astype(BF16).reshape(8, 32, HALF)
        send1[h, 8:16] = odd.astype(BF16).reshape(8, 32, HALF)
        if h == 0:
            pl.semaphore_wait(barrier, 67)

        @pl.loop(1, 16)
        def _(k):
            to, slot = zy_partner(k)
            pltpu.make_async_remote_copy(
                send1.at[h, slot], recv1.at[h, mine1], ssem.at[h], rsem.at[h],
                device_id=(to, col), device_id_type=MESH,
            ).start()

        recv1[h, mine1] = send1[h, mine1]

    constants[0].wait()
    constants[1].wait()
    lane_c = lax.broadcasted_iota(jnp.int32, (GROUP, HALF), 1) % GROUP
    row_c = lax.broadcasted_iota(jnp.int32, (GROUP, HALF), 0)
    pick = jnp.where(lane_c == row_c, 1.0, 0.0).astype(BF16)
    for h in range(2):
        arrived = recv1.at[h, pl.ds(0, 15)]
        pltpu.make_async_copy(arrived, arrived, rsem.at[h]).wait()
        lanes = pl.ds(h * HALF, HALF)
        data = recv1[h].reshape(512, HALF)
        cosine, sine = ftw_v[0, :, lanes], ftw_v[1, :, lanes]
        for block in range(4):
            part = jnp.dot(fxt_v[pl.ds(block * 256, 256), :], data, preferred_element_type=F32)
            part = part.reshape(2, 4, KX, HALF)
            real, imag = part[0], part[1]
            turned = jnp.concatenate([
                real * cosine + imag * sine,
                imag * cosine - real * sine,
            ]).reshape(256, HALF).astype(BF16)
            summed = lax.dot_general(pick, turned, NT, preferred_element_type=F32)
            if h == 0:
                partial[block] = summed
            else:
                send2[block] = (partial[block] + summed).astype(BF16)

    mine2 = col * 4 + xlo * 2 + core

    @pl.loop(1, 8)
    def _(k):
        to, col2, block = near_partner(k)
        pltpu.make_async_remote_copy(
            send2.at[block], recv2.at[mine2], ssem.at[2], rsem.at[2],
            device_id=(to, col2), device_id_type=MESH,
        ).start()

    recv2[mine2] = send2[xlo * 2 + core]
    for copy in constants[2:]:
        copy.wait()
    arrived = recv2.at[pl.ds(0, 7)]
    pltpu.make_async_copy(arrived, arrived, rsem.at[2]).wait()
    for c in range(2):
        total = recv2[c * 4].astype(F32)
        for k in range(1, 4):
            total += recv2[c * 4 + k].astype(F32)
        total = total.astype(BF16).astype(F32)
        modes[0, pl.ds(c * GROUP, GROUP), :] = total[:, 0:128]
        modes[1, pl.ds(c * GROUP, GROUP), :] = total[:, 128:256]

    def mix(step, sums):
        real, imag = sums
        rows = pl.ds(pl.multiple_of(step * 8, 8), 8)
        mrs, mis = modes[0, rows, :], modes[1, rows, :]
        for k in range(8):
            mr, mi = mrs[k:k + 1], mis[k:k + 1]
            wr, wi = wbuf[0, step * 8 + k].astype(F32), wbuf[1, step * 8 + k].astype(F32)
            real, imag = real + (wr * mr - wi * mi), imag + (wr * mi + wi * mr)
        return real, imag

    zero = jnp.zeros((GROUP, 128), F32)
    real, imag = lax.fori_loop(0, 8, mix, (zero, zero))
    mixed = jnp.concatenate([real, imag], axis=1).astype(BF16)
    spread = lax.dot_general(mixed, pick, TN, preferred_element_type=F32)
    cosine, sine = itw_v[0], itw_v[1]
    real, imag = spread[0:128], spread[128:256]
    turned = jnp.concatenate([
        real * cosine - imag * sine,
        real * sine + imag * cosine,
    ]).astype(BF16)
    for q in range(4):
        rows = jnp.dot(ixt_v[pl.ds(q * 256, 256), :], turned, preferred_element_type=F32)
        send3[pl.ds(q * 16, 16)] = rows.astype(BF16).reshape(16, 16, HALF)

    mine3 = (y % 2) * 32 + (z * 2 + y // 2) * 4 + xlo * 2 + core

    @pl.loop(1, 64)
    def _(k):
        to = (g + k) % 64
        pltpu.make_async_remote_copy(
            send3.at[to], recv3.at[mine3], ssem.at[3], rsem.at[3],
            device_id=(to, col), device_id_type=MESH,
        ).start()

    recv3[mine3] = send3[g]
    arrived = recv3.at[pl.ds(0, 63)]
    pltpu.make_async_copy(arrived, arrived, rsem.at[3]).wait()
    out[...] = recv3[...]
    for h in range(2):
        sent = send1.at[h, pl.ds(0, 15)]
        pltpu.make_async_copy(sent, sent, ssem.at[h]).wait()
    sent = recv2.at[pl.ds(0, 7)]
    pltpu.make_async_copy(sent, sent, ssem.at[2]).wait()
    sent = send3.at[pl.ds(0, 63)]
    pltpu.make_async_copy(sent, sent, ssem.at[3]).wait()


def finish_kernel(slabs, table, state, gain, bias, out, vals, tbuf, xbuf, obuf, tsem, xsem, osem):
    steps = FOLD // STEP

    def load(j):
        at = pl.ds(j * STEP, STEP)
        slot = j % 2
        copies = [pltpu.make_async_copy(table.at[:, at], tbuf.at[slot], tsem.at[slot])]
        for s in range(2):
            at = pl.ds(s * FOLD + j * STEP, STEP)
            copies.append(pltpu.make_async_copy(state.at[:, at], xbuf.at[slot, s], xsem.at[slot, s]))
        return copies

    def store(j):
        slot = j % 2
        return [
            pltpu.make_async_copy(
                obuf.at[slot, s], out.at[:, pl.ds(s * FOLD + j * STEP, STEP)], osem.at[slot, s]
            )
            for s in range(2)
        ]

    for copy in load(0):
        copy.start()
    for h in range(2):
        part = slabs[...].astype(F32)[:, h * 8:(h + 1) * 8, :].reshape(512, HALF)
        vals[pl.ds(h * HALF, HALF), :] = part.T.astype(BF16)
    square = (GROUP, GROUP)
    diagonal = lax.broadcasted_iota(jnp.int32, square, 0) == lax.broadcasted_iota(jnp.int32, square, 1)
    gain_c = 0.5 * jnp.sum(jnp.where(diagonal, gain[...], 0.0), axis=1, keepdims=True)
    bias_c = 0.5 * jnp.sum(jnp.where(diagonal, bias[...], 0.0), axis=1, keepdims=True)
    c1 = 2.0 * math.sqrt(2.0 / math.pi)
    c3 = 8.0 * 0.044715 * math.sqrt(2.0 / math.pi)
    for j in range(steps):
        slot = j % 2
        if j + 1 < steps:
            for copy in load(j + 1):
                copy.start()
        for copy in load(j):
            copy.wait()
        if j >= 2:
            for copy in store(j - 2):
                copy.wait()

        @pl.loop(0, ROWS // 128)
        def _(m):
            rows = pl.ds(pl.multiple_of(m * 128, 128), 128)
            even = jnp.dot(vals[rows, 0:256], tbuf[slot, 0:256, :], preferred_element_type=F32)
            odd = jnp.dot(vals[rows, 256:512], tbuf[slot, 256:512, :], preferred_element_type=F32)
            for s in range(2):
                spectral = even + odd if s == 0 else even - odd
                local = xbuf[slot, s, rows, :].astype(F32).reshape(4, GROUP, STEP)
                v = spectral.reshape(4, GROUP, STEP) + (local * gain_c + bias_c)
                u = v * (c1 + c3 * (v * v))
                res = v + v * jnp.tanh(u)
                obuf[slot, s, rows, :] = res.reshape(128, STEP).astype(BF16)

        for copy in store(j):
            copy.start()
    for j in (steps - 2, steps - 1):
        for copy in store(j):
            copy.wait()


def shards(state_field, spectral_weight, local_weight, channel_bias):
    state = state_field.reshape(ROWS, PLANE)
    table = jnp.asarray(plane_table())
    anywhere = pl.BlockSpec(memory_space=pl.ANY)
    vmem = pl.BlockSpec(memory_space=pltpu.VMEM)
    slabs = pl.pallas_call(
        exchange_kernel,
        out_shape=jax.ShapeDtypeStruct((64, 16, HALF), BF16),
        in_specs=[anywhere] * 7,
        out_specs=vmem,
        scratch_shapes=[
            pltpu.VMEM((ROWS, PLANE), BF16),
            pltpu.VMEM((512, FOLD), BF16),
            pltpu.VMEM((2, 64, GROUP, 128), BF16),
            pltpu.VMEM((1024, 512), BF16),
            pltpu.VMEM((2, KX, ROWS), F32),
            pltpu.VMEM((1024, 256), BF16),
            pltpu.VMEM((2, 128, HALF), F32),
            pltpu.VMEM((2, 16, 32, HALF), BF16),
            pltpu.VMEM((2, 16, 32, HALF), BF16),
            pltpu.VMEM((4, GROUP, 256), F32),
            pltpu.VMEM((4, GROUP, 256), BF16),
            pltpu.VMEM((8, GROUP, 256), BF16),
            pltpu.VMEM((2, 64, 128), F32),
            pltpu.VMEM((64, 16, HALF), BF16),
            pltpu.VMEM((64, 16, HALF), BF16),
            pltpu.SemaphoreType.DMA((PIECES,)),
            pltpu.SemaphoreType.DMA((4 * PIECES,)),
            pltpu.SemaphoreType.DMA((5,)),
            pltpu.SemaphoreType.DMA((4,)),
            pltpu.SemaphoreType.DMA((4,)),
        ],
        compiler_params=pltpu.CompilerParams(
            collective_id=0, has_side_effects=True, vmem_limit_bytes=48 << 20
        ),
        name="exchange",
    )(
        state,
        spectral_weight,
        table,
        jnp.asarray(forward_x_table()),
        jnp.asarray(forward_twiddle()),
        jnp.asarray(inverse_x_table()),
        jnp.asarray(inverse_twiddle()),
    )
    result = pl.pallas_call(
        finish_kernel,
        out_shape=jax.ShapeDtypeStruct((ROWS, PLANE), BF16),
        in_specs=[vmem, anywhere, anywhere, vmem, vmem],
        out_specs=anywhere,
        scratch_shapes=[
            pltpu.VMEM((ROWS, 512), BF16),
            pltpu.VMEM((2, 512, STEP), BF16),
            pltpu.VMEM((2, 2, ROWS, STEP), BF16),
            pltpu.VMEM((2, 2, ROWS, STEP), BF16),
            pltpu.SemaphoreType.DMA((2,)),
            pltpu.SemaphoreType.DMA((2, 2)),
            pltpu.SemaphoreType.DMA((2, 2)),
        ],
        compiler_params=pltpu.CompilerParams(vmem_limit_bytes=32 << 20),
        name="finish",
    )(slabs, table, state, local_weight.reshape(1, GROUP), channel_bias.reshape(1, GROUP))
    return result.reshape(state_field.shape)


def solution(mesh):
    return jax.shard_map(
        shards,
        mesh=mesh,
        in_specs=(P("gx", "col", None), P(None, None, "col", "gx"), P("col"), P("col")),
        out_specs=P("gx", "col", None),
        check_vma=False,
    )
```

```python
import math

import jax
import jax.numpy as jnp
import ml_dtypes
import numpy as np
from jax import lax
from jax.experimental import pallas as pl
from jax.experimental.pallas import tpu as pltpu
from jax.sharding import PartitionSpec as P

MESH = pl.DeviceIdType.MESH
BF16 = jnp.bfloat16
F32 = jnp.float32

XCELLS = 1024
YCELLS = 128
TSTEPS = 64
KX = 32
KY = 32
KT = 8
PLANE = YCELLS * TSTEPS
FOLD = PLANE // 2
SLABS = 64
XDEV = 16
GROUP = 32
ROWS = XDEV * GROUP
HALF = ROWS // 2
PIECES = 4
PIECE = FOLD // PIECES
STEP = 512
BLOCK = 256
MB = 64
PRE = 256

NT = (((1,), (1,)), ((), ()))
TN = (((0,), (0,)), ((), ()))


def freq(index, number):
    return np.where(index < number // 2, index, index - number)


def plane_table():
    p, z, yh, xlo, half, r, kt4 = np.meshgrid(
        *[np.arange(n) for n in (2, 4, 2, 2, 2, 2, 4)], indexing="ij"
    )
    ky = freq((z * 8 + xlo * 4 + yh * 2 + p).reshape(-1), KY)
    kt = (half * 4 + kt4).reshape(-1)
    r = r.reshape(-1)
    cells = np.arange(FOLD)
    y, t = cells // TSTEPS, cells % TSTEPS
    phase = (ky[:, None] * y[None] * TSTEPS + kt[:, None] * t[None] * YCELLS) % PLANE
    angle = phase * (2.0 * math.pi / PLANE)
    table = np.where(r[:, None] == 0, np.cos(angle), -np.sin(angle))
    return table.astype(ml_dtypes.bfloat16)


def forward_x_table():
    kx = freq(np.arange(KX), KX)
    slot = np.arange(16)
    p, z, yh = slot // 8, (slot // 2) % 4, slot % 2
    angle = 2.0 * math.pi * ((kx[:, None] * (8 * z + yh * 2 + p)[None]) % 32) / 32
    cosine, sine = np.cos(angle), np.sin(angle)
    table = np.zeros((4, 2, 4, KX, 16, 4, 2, 4))
    for block in range(4):
        for k in range(4):
            table[block, 0, k, :, :, block, 0, k] = cosine
            table[block, 0, k, :, :, block, 1, k] = sine
            table[block, 1, k, :, :, block, 1, k] = cosine
            table[block, 1, k, :, :, block, 0, k] = -sine
    return table.reshape(1024, 512).astype(ml_dtypes.bfloat16)


def forward_twiddle():
    kx = freq(np.arange(KX), KX)
    scale = 1.0 / math.sqrt(XCELLS * PLANE)
    place = np.arange(4)
    offset = (place // 2) * 128 + (place % 2) * 16
    lanes = np.arange(ROWS) // GROUP
    angle = 2.0 * math.pi * ((kx[None, :, None] * (offset[:, None, None] + lanes)) % XCELLS) / XCELLS
    return (np.stack([np.cos(angle), np.sin(angle)], axis=1) * scale).astype(np.float32)


def inverse_x_table():
    kx = freq(np.arange(KX), KX)
    angle = 2.0 * math.pi * ((kx[None] * (8 * np.arange(128))[:, None]) % XCELLS) / XCELLS
    cosine, sine = np.cos(angle), np.sin(angle)
    table = np.zeros((128, 2, 4, 2, 4, KX))
    for k in range(4):
        table[:, 0, k, 0, k] = cosine
        table[:, 0, k, 1, k] = -sine
        table[:, 1, k, 0, k] = sine
        table[:, 1, k, 1, k] = cosine
    return table.reshape(1024, 256).astype(ml_dtypes.bfloat16)


def inverse_twiddle():
    kx = np.tile(freq(np.arange(KX), KX), 4)
    kt4 = np.repeat(np.arange(4), KX)
    lanes = np.arange(HALF) // GROUP
    angle = 2.0 * math.pi * ((kx[:, None] * lanes[None]) % XCELLS) / XCELLS
    parts = np.stack([np.cos(angle), np.sin(angle)])
    weight = np.stack([np.where(kt4 + 4 * half == 0, 1.0, 2.0) for half in range(2)])
    scale = 0.5 / math.sqrt(PLANE)
    return (parts[None] * weight[:, None, :, None] * scale).astype(np.float32)


def place_of(g):
    return g // 16, (g // 8) % 2, (g // 2) % 4, g % 2


def exchange_kernel(
    state, weight, gain, bias, table, fxt, ftw, ixt, itw, out, pre, tbuf,
    xbuf, wbuf, gain_v, bias_v, fxt_v, ftw_v, ixt_v, itw_v,
    send1, recv1, partial, send2, recv2, modes, send3, recv3,
    tsem, xsem, csem, ssem, rsem,
):
    g = lax.axis_index("gx")
    col = lax.axis_index("col")
    z, xlo, y, core = place_of(g)

    def zy_partner(k):
        z2, y2 = (z + k // 4) % 4, (y + k % 4) % 4
        return z2 * 16 + xlo * 8 + y2 * 2 + core, (y2 % 2) * 8 + z2 * 2 + y2 // 2

    def near_partner(k):
        xlo2, core2, col2 = (xlo + (k // 2) % 2) % 2, (core + k % 2) % 2, (col + k // 4) % 2
        return z * 16 + xlo2 * 8 + y * 2 + core2, col2, xlo2 * 2 + core2

    loads = []
    for k in range(PIECES):
        cols = pl.ds(k * PIECE, PIECE)
        loads.append(pltpu.make_async_copy(table.at[:, cols], tbuf.at[:, cols], tsem.at[k]))
        loads[-1].start()
        for s in range(2):
            at = pl.ds(s * FOLD + k * PIECE, PIECE)
            pltpu.make_async_copy(
                state.at[pl.ds(0, HALF), at], xbuf.at[pl.ds(0, HALF), at], xsem.at[k * 2 + s]
            ).start()
    for k in range(PIECES):
        for s in range(2):
            at = pl.ds(s * FOLD + k * PIECE, PIECE)
            pltpu.make_async_copy(
                state.at[pl.ds(HALF, HALF), at],
                xbuf.at[pl.ds(HALF, HALF), at],
                xsem.at[2 * PIECES + k * 2 + s],
            ).start()
    constants = [
        pltpu.make_async_copy(fxt, fxt_v, csem.at[0]),
        pltpu.make_async_copy(ftw.at[xlo * 2 + core], ftw_v, csem.at[1]),
        pltpu.make_async_copy(weight, wbuf, csem.at[2]),
        pltpu.make_async_copy(itw.at[core], itw_v, csem.at[3]),
        pltpu.make_async_copy(ixt, ixt_v, csem.at[4]),
    ]
    local_copies = [
        pltpu.make_async_copy(gain, gain_v, csem.at[5]),
        pltpu.make_async_copy(bias, bias_v, csem.at[6]),
    ]
    for copy in constants + local_copies:
        copy.start()

    square = (GROUP, GROUP)
    diagonal = lax.broadcasted_iota(jnp.int32, square, 0) == lax.broadcasted_iota(jnp.int32, square, 1)

    def column(row):
        part = 0.5 * jnp.sum(jnp.where(diagonal, row, 0.0), axis=1, keepdims=True)
        return jnp.broadcast_to(part, (GROUP, PRE))


    barrier = pltpu.get_barrier_semaphore()

    @pl.loop(1, 64)
    def _(k):
        pl.semaphore_signal(barrier, inc=1, device_id=((g + k) % 64, col), device_id_type=MESH)

    @pl.loop(4, 8)
    def _(k):
        to, col2, _slot = near_partner(k)
        pl.semaphore_signal(barrier, inc=1, device_id=(to, col2), device_id_type=MESH)

    mine1 = (y % 2) * 8 + z * 2 + y // 2
    for h in range(2):
        rows = pl.ds(h * HALF, HALF)
        even = jnp.zeros((256, HALF), F32)
        odd = jnp.zeros((256, HALF), F32)
        for k in range(PIECES):
            lo = pl.ds(k * PIECE, PIECE)
            hi = pl.ds(FOLD + k * PIECE, PIECE)
            if h == 0:
                loads[k].wait()
            for s, at in ((0, lo), (1, hi)):
                pltpu.make_async_copy(
                    state.at[rows, at], xbuf.at[rows, at], xsem.at[h * 2 * PIECES + k * 2 + s]
                ).wait()
            x0, x1 = xbuf[rows, lo], xbuf[rows, hi]
            even += lax.dot_general(tbuf[0:256, lo], x0 + x1, NT, preferred_element_type=F32)
            odd += lax.dot_general(tbuf[256:512, lo], x0 - x1, NT, preferred_element_type=F32)
        send1[h, 0:8] = even.astype(BF16).reshape(8, 32, HALF)
        send1[h, 8:16] = odd.astype(BF16).reshape(8, 32, HALF)
        if h == 0:
            pl.semaphore_wait(barrier, 67)

        @pl.loop(1, 16)
        def _(k):
            to, slot = zy_partner(k)
            pltpu.make_async_remote_copy(
                send1.at[h, slot], recv1.at[h, mine1], ssem.at[h], rsem.at[h],
                device_id=(to, col), device_id_type=MESH,
            ).start()

        recv1[h, mine1] = send1[h, mine1]

    local_copies[0].wait()
    local_copies[1].wait()
    gain_c, bias_c = column(gain_v[...]), column(bias_v[...])

    @pl.loop(0, XDEV)
    def _(x):
        rows = pl.ds(pl.multiple_of(x * GROUP, GROUP), GROUP)
        for at in range(0, PLANE, PRE):
            pre[rows, pl.ds(at, PRE)] = xbuf[rows, pl.ds(at, PRE)].astype(F32) * gain_c + bias_c

    constants[0].wait()
    constants[1].wait()
    lane_c = lax.broadcasted_iota(jnp.int32, (GROUP, HALF), 1) % GROUP
    row_c = lax.broadcasted_iota(jnp.int32, (GROUP, HALF), 0)
    pick = jnp.where(lane_c == row_c, 1.0, 0.0).astype(BF16)
    for h in range(2):
        arrived = recv1.at[h, pl.ds(0, 15)]
        pltpu.make_async_copy(arrived, arrived, rsem.at[h]).wait()
        lanes = pl.ds(h * HALF, HALF)
        data = recv1[h].reshape(512, HALF)
        cosine, sine = ftw_v[0, :, lanes], ftw_v[1, :, lanes]
        for block in range(4):
            part = jnp.dot(fxt_v[pl.ds(block * 256, 256), :], data, preferred_element_type=F32)
            part = part.reshape(2, 4, KX, HALF)
            real, imag = part[0], part[1]
            turned = jnp.concatenate([
                real * cosine + imag * sine,
                imag * cosine - real * sine,
            ]).reshape(256, HALF).astype(BF16)
            summed = lax.dot_general(pick, turned, NT, preferred_element_type=F32)
            if h == 0:
                partial[block] = summed
            else:
                send2[block] = (partial[block] + summed).astype(BF16)

    mine2 = col * 4 + xlo * 2 + core

    @pl.loop(1, 8)
    def _(k):
        to, col2, block = near_partner(k)
        pltpu.make_async_remote_copy(
            send2.at[block], recv2.at[mine2], ssem.at[2], rsem.at[2],
            device_id=(to, col2), device_id_type=MESH,
        ).start()

    recv2[mine2] = send2[xlo * 2 + core]
    for copy in constants[2:]:
        copy.wait()
    arrived = recv2.at[pl.ds(0, 7)]
    pltpu.make_async_copy(arrived, arrived, rsem.at[2]).wait()
    for c in range(2):
        total = recv2[c * 4].astype(F32)
        for k in range(1, 4):
            total += recv2[c * 4 + k].astype(F32)
        total = total.astype(BF16).astype(F32)
        modes[0, pl.ds(c * GROUP, GROUP), :] = total[:, 0:128]
        modes[1, pl.ds(c * GROUP, GROUP), :] = total[:, 128:256]

    def mix(step, sums):
        real, imag = sums
        rows = pl.ds(pl.multiple_of(step * 8, 8), 8)
        mrs, mis = modes[0, rows, :], modes[1, rows, :]
        for k in range(8):
            mr, mi = mrs[k:k + 1], mis[k:k + 1]
            wr, wi = wbuf[0, step * 8 + k].astype(F32), wbuf[1, step * 8 + k].astype(F32)
            real, imag = real + (wr * mr - wi * mi), imag + (wr * mi + wi * mr)
        return real, imag

    zero = jnp.zeros((GROUP, 128), F32)
    real, imag = lax.fori_loop(0, 8, mix, (zero, zero))
    mixed = jnp.concatenate([real, imag], axis=1).astype(BF16)
    spread = lax.dot_general(mixed, pick, TN, preferred_element_type=F32)
    cosine, sine = itw_v[0], itw_v[1]
    real, imag = spread[0:128], spread[128:256]
    turned = jnp.concatenate([
        real * cosine - imag * sine,
        real * sine + imag * cosine,
    ]).astype(BF16)
    for q in range(4):
        rows = jnp.dot(ixt_v[pl.ds(q * 256, 256), :], turned, preferred_element_type=F32)
        send3[pl.ds(q * 16, 16)] = rows.astype(BF16).reshape(16, 16, HALF)

    mine3 = (y % 2) * 32 + (z * 2 + y // 2) * 4 + xlo * 2 + core

    @pl.loop(1, 64)
    def _(k):
        to = (g + k) % 64
        pltpu.make_async_remote_copy(
            send3.at[to], recv3.at[mine3], ssem.at[3], rsem.at[3],
            device_id=(to, col), device_id_type=MESH,
        ).start()

    recv3[mine3] = send3[g]
    arrived = recv3.at[pl.ds(0, 63)]
    pltpu.make_async_copy(arrived, arrived, rsem.at[3]).wait()
    out[...] = recv3[...]
    for h in range(2):
        sent = send1.at[h, pl.ds(0, 15)]
        pltpu.make_async_copy(sent, sent, ssem.at[h]).wait()
    sent = recv2.at[pl.ds(0, 7)]
    pltpu.make_async_copy(sent, sent, ssem.at[2]).wait()
    sent = send3.at[pl.ds(0, 63)]
    pltpu.make_async_copy(sent, sent, ssem.at[3]).wait()


def finish_kernel(slabs, pre, table, out, vals, obuf, evens, odds, osem):
    c1 = 2.0 * math.sqrt(2.0 / math.pi)
    c3 = 8.0 * 0.044715 * math.sqrt(2.0 / math.pi)

    def store(j):
        return [
            pltpu.make_async_copy(
                obuf.at[j % 2, s], out.at[:, pl.ds(s * FOLD + j * STEP, STEP)], osem.at[j % 2, s]
            )
            for s in range(2)
        ]

    def products(n):
        cols = pl.ds(n * BLOCK, BLOCK)
        evens[n % 2] = jnp.dot(vals[:, 0:256], table[0:256, cols], preferred_element_type=F32)
        odds[n % 2] = jnp.dot(vals[:, 256:512], table[256:512, cols], preferred_element_type=F32)

    for h in range(2):
        part = slabs[...].astype(F32)[:, h * 8:(h + 1) * 8, :].reshape(512, HALF)
        vals[pl.ds(h * HALF, HALF), :] = part.T.astype(BF16)
    products(0)
    steps = FOLD // STEP
    for j in range(steps):
        if j >= 2:
            for copy in store(j - 2):
                copy.wait()
        for i in range(STEP // BLOCK):
            n = j * (STEP // BLOCK) + i
            if (n + 1) * BLOCK < FOLD:
                products(n + 1)
            for m in range(ROWS // MB):
                rows = pl.ds(m * MB, MB)
                even, odd = evens[n % 2, rows, :], odds[n % 2, rows, :]
                for s in range(2):
                    spectral = even + odd if s == 0 else even - odd
                    v = spectral + pre[rows, pl.ds(s * FOLD + n * BLOCK, BLOCK)]
                    u = v * (c1 + c3 * (v * v))
                    obuf[j % 2, s, rows, pl.ds(i * BLOCK, BLOCK)] = (v + v * jnp.tanh(u)).astype(BF16)
        for copy in store(j):
            copy.start()
    for j in (steps - 2, steps - 1):
        for copy in store(j):
            copy.wait()


def in_hbm(array):
    return pltpu.with_memory_space_constraint(array, pltpu.HBM)


def shards(state_field, spectral_weight, local_weight, channel_bias):
    state = state_field.reshape(ROWS, PLANE)
    anywhere = pl.BlockSpec(memory_space=pltpu.HBM)
    vmem = pl.BlockSpec(memory_space=pltpu.VMEM)
    slabs, pre, table_v = pl.pallas_call(
        exchange_kernel,
        out_shape=[
            jax.ShapeDtypeStruct((64, 16, HALF), BF16),
            jax.ShapeDtypeStruct((ROWS, PLANE), F32),
            jax.ShapeDtypeStruct((512, FOLD), BF16),
        ],
        in_specs=[anywhere] * 9,
        out_specs=[vmem] * 3,
        scratch_shapes=[
            pltpu.VMEM((ROWS, PLANE), BF16),
            pltpu.VMEM((2, 64, GROUP, 128), BF16),
            pltpu.VMEM((1, GROUP), F32),
            pltpu.VMEM((1, GROUP), F32),
            pltpu.VMEM((1024, 512), BF16),
            pltpu.VMEM((2, KX, ROWS), F32),
            pltpu.VMEM((1024, 256), BF16),
            pltpu.VMEM((2, 128, HALF), F32),
            pltpu.VMEM((2, 16, 32, HALF), BF16),
            pltpu.VMEM((2, 16, 32, HALF), BF16),
            pltpu.VMEM((4, GROUP, 256), F32),
            pltpu.VMEM((4, GROUP, 256), BF16),
            pltpu.VMEM((8, GROUP, 256), BF16),
            pltpu.VMEM((2, 64, 128), F32),
            pltpu.VMEM((64, 16, HALF), BF16),
            pltpu.VMEM((64, 16, HALF), BF16),
            pltpu.SemaphoreType.DMA((PIECES,)),
            pltpu.SemaphoreType.DMA((4 * PIECES,)),
            pltpu.SemaphoreType.DMA((7,)),
            pltpu.SemaphoreType.DMA((4,)),
            pltpu.SemaphoreType.DMA((4,)),
        ],
        compiler_params=pltpu.CompilerParams(
            collective_id=0, has_side_effects=True, vmem_limit_bytes=20 << 20
        ),
        name="exchange",
    )(
        in_hbm(state),
        in_hbm(spectral_weight),
        in_hbm(local_weight.reshape(1, GROUP)),
        in_hbm(channel_bias.reshape(1, GROUP)),
        *[in_hbm(jnp.asarray(table())) for table in (
            plane_table, forward_x_table, forward_twiddle, inverse_x_table, inverse_twiddle
        )],
    )
    result = pl.pallas_call(
        finish_kernel,
        out_shape=jax.ShapeDtypeStruct((ROWS, PLANE), BF16),
        in_specs=[vmem] * 3,
        out_specs=anywhere,
        scratch_shapes=[
            pltpu.VMEM((ROWS, 512), BF16),
            pltpu.VMEM((2, 2, ROWS, STEP), BF16),
            pltpu.VMEM((2, ROWS, BLOCK), F32),
            pltpu.VMEM((2, ROWS, BLOCK), F32),
            pltpu.SemaphoreType.DMA((2, 2)),
        ],
        compiler_params=pltpu.CompilerParams(vmem_limit_bytes=16 << 20),
        name="finish",
    )(slabs, pre, table_v)
    return result.reshape(state_field.shape)


def solution(mesh):
    return jax.shard_map(
        shards,
        mesh=mesh,
        in_specs=(P("gx", "col", None), P(None, None, "col", "gx"), P("col"), P("col")),
        out_specs=P("gx", "col", None),
        check_vma=False,
    )
```

```python
import math

import jax
import jax.numpy as jnp
import ml_dtypes
import numpy as np
from jax import lax
from jax.experimental import pallas as pl
from jax.experimental.pallas import tpu as pltpu
from jax.sharding import PartitionSpec as P

MESH = pl.DeviceIdType.MESH
BF16 = jnp.bfloat16
F32 = jnp.float32

XCELLS = 1024
YCELLS = 128
TSTEPS = 64
KX = 32
KY = 32
PLANE = YCELLS * TSTEPS
FOLD = PLANE // 2
QUARTER = PLANE // 4
XDEV = 16
GROUP = 32
ROWS = XDEV * GROUP
HALF = ROWS // 2
PIECES = 4
PIECE = FOLD // PIECES
STEP = 512
BLOCK = 256
MB = 64
PRE = 256

NT = (((1,), (1,)), ((), ()))
TN = (((0,), (0,)), ((), ()))


FAR_FIRST = sorted(
    [(dz, dy) for dz in range(4) for dy in range(4) if dz or dy],
    key=lambda o: -(min(o[0], 4 - o[0]) + min(o[1], 4 - o[1])),
)


def freq(index, number):
    return np.where(index < number // 2, index, index - number)


def plane_table():
    p, c, z, yh, xlo, half, r, kt2 = np.meshgrid(
        *[np.arange(n) for n in (2, 2, 4, 2, 2, 2, 2, 2)], indexing="ij"
    )
    ky = freq((z * 8 + xlo * 4 + yh * 2 + p).reshape(-1), KY)
    kt = (half * 4 + c * 2 + kt2).reshape(-1)
    r = r.reshape(-1)
    cells = np.arange(FOLD)
    y, t = cells // TSTEPS, cells % TSTEPS
    phase = (ky[:, None] * y[None] * TSTEPS + kt[:, None] * t[None] * YCELLS) % PLANE
    angle = phase * (2.0 * math.pi / PLANE)
    table = np.where(r[:, None] == 0, np.cos(angle), -np.sin(angle))
    return table.astype(ml_dtypes.bfloat16)


def forward_x_table():
    kx = freq(np.arange(KX), KX)
    slot = np.arange(16)
    p, z, yh = slot // 8, (slot // 2) % 4, slot % 2
    angle = 2.0 * math.pi * ((kx[:, None] * (8 * z + yh * 2 + p)[None]) % 32) / 32
    cosine, sine = np.cos(angle), np.sin(angle)
    table = np.zeros((4, 2, 2, KX, 16, 4, 2, 2))
    for block in range(4):
        for k in range(2):
            table[block, 0, k, :, :, block, 0, k] = cosine
            table[block, 0, k, :, :, block, 1, k] = sine
            table[block, 1, k, :, :, block, 1, k] = cosine
            table[block, 1, k, :, :, block, 0, k] = -sine
    return table.reshape(512, 256).astype(ml_dtypes.bfloat16)


def forward_twiddle():
    kx = freq(np.arange(KX), KX)
    scale = 1.0 / math.sqrt(XCELLS * PLANE)
    place = np.arange(4)
    offset = (place // 2) * 128 + (place % 2) * 16
    lanes = np.arange(ROWS) // GROUP
    angle = 2.0 * math.pi * ((kx[None, :, None] * (offset[:, None, None] + lanes)) % XCELLS) / XCELLS
    return (np.stack([np.cos(angle), np.sin(angle)], axis=1) * scale).astype(np.float32)


def inverse_x_table():
    kx = freq(np.arange(KX), KX)
    angle = 2.0 * math.pi * ((kx[None] * (4 * np.arange(256))[:, None]) % XCELLS) / XCELLS
    cosine, sine = np.cos(angle), np.sin(angle)
    table = np.zeros((256, 2, 2, 2, 2, KX))
    for k in range(2):
        table[:, 0, k, 0, k] = cosine
        table[:, 0, k, 1, k] = -sine
        table[:, 1, k, 0, k] = sine
        table[:, 1, k, 1, k] = cosine
    return table.reshape(1024, 128).astype(ml_dtypes.bfloat16)


def inverse_twiddle():
    kx = np.tile(freq(np.arange(KX), KX), 2)
    kt2 = np.repeat(np.arange(2), KX)
    lanes = np.arange(128) // GROUP
    angle = 2.0 * math.pi * ((kx[:, None] * lanes[None]) % XCELLS) / XCELLS
    parts = np.stack([np.cos(angle), np.sin(angle)])
    weight = np.stack([np.where(kt2 + 2 * other == 0, 1.0, 2.0) for other in range(2)])
    scale = 0.5 / math.sqrt(PLANE)
    return (parts[None] * weight[:, None, :, None] * scale).astype(np.float32)


def place_of(g):
    return g // 16, (g // 8) % 2, (g // 2) % 4, g % 2


def exchange_kernel(
    state, weight, gain, bias, table, fxt, ftw, ixt, itw, out, pre, tbuf,
    xbuf, wbuf, gain_v, bias_v, fxt_v, ftw_v, ixt_v, itw_v, wmix,
    send1, recv1, send2, recv2, modes, send3, recv3,
    tsem, xsem, csem, ssem, rsem,
):
    g = lax.axis_index("gx")
    col = lax.axis_index("col")
    z, xlo, y, core = place_of(g)

    def zy_partner(dz, dy):
        z2, y2 = (z + dz) % 4, (y + dy) % 4
        return z2 * 16 + xlo * 8 + y2 * 2 + core, (y2 % 2) * 8 + z2 * 2 + y2 // 2

    def near_partner(k):
        xlo2, core2, col2 = (xlo + k % 2) % 2, (core + (k // 2) % 2) % 2, (col + k // 4) % 2
        return z * 16 + xlo2 * 8 + y * 2 + core2, col2, xlo2 * 2 + core2

    def wait_bytes(ref, sem):
        pltpu.make_async_copy(ref, ref, sem).wait()

    table_loads = []
    for k in range(2):
        cols = pl.ds(k * PIECE, PIECE)
        table_loads.append(pltpu.make_async_copy(table.at[:, cols], tbuf.at[:, cols], tsem.at[k]))
    rest = pl.ds(QUARTER, QUARTER)
    table_loads.append(pltpu.make_async_copy(table.at[:, rest], tbuf.at[:, rest], tsem.at[2]))
    state_loads = {}
    for h in range(2):
        for k in range(PIECES):
            for s in range(2):
                rows, at = pl.ds(h * HALF, HALF), pl.ds(s * FOLD + k * PIECE, PIECE)
                state_loads[h, k, s] = pltpu.make_async_copy(
                    state.at[rows, at], xbuf.at[rows, at], xsem.at[(h * PIECES + k) * 2 + s]
                )
    for k in range(PIECES):
        if k < 2:
            table_loads[k].start()
        for s in range(2):
            state_loads[0, k, s].start()
    constants = [
        pltpu.make_async_copy(gain, gain_v, csem.at[0]),
        pltpu.make_async_copy(bias, bias_v, csem.at[1]),
        pltpu.make_async_copy(weight, wbuf, csem.at[2]),
        pltpu.make_async_copy(fxt, fxt_v, csem.at[3]),
        pltpu.make_async_copy(ftw.at[xlo * 2 + core], ftw_v, csem.at[4]),
        pltpu.make_async_copy(itw, itw_v, csem.at[5]),
        pltpu.make_async_copy(ixt, ixt_v, csem.at[6]),
        table_loads[2],
    ]

    barrier = pltpu.get_barrier_semaphore()

    @pl.loop(1, 64)
    def _(k):
        pl.semaphore_signal(barrier, inc=1, device_id=((g + k) % 64, col), device_id_type=MESH)

    @pl.loop(4, 8)
    def _(k):
        to, col2, _slot = near_partner(k)
        pl.semaphore_signal(barrier, inc=1, device_id=(to, col2), device_id_type=MESH)

    row4 = lax.broadcasted_iota(jnp.int32, (256, HALF), 0) % 4
    mine1 = (y % 2) * 8 + z * 2 + y // 2
    for h in range(2):
        rows = pl.ds(h * HALF, HALF)
        sums = [[None, None], [None, None]]
        for k in range(PIECES):
            lo = pl.ds(k * PIECE, PIECE)
            hi = pl.ds(FOLD + k * PIECE, PIECE)
            cols = pl.ds((k % 2) * PIECE, PIECE)
            if h == 0 and k < 2:
                table_loads[k].wait()
            for s in range(2):
                state_loads[h, k, s].wait()
                if h == 0:
                    state_loads[1, k, s].start()
            x0, x1 = xbuf[rows, lo], xbuf[rows, hi]
            for p, x in ((0, x0 + x1), (1, x0 - x1)):
                part = lax.dot_general(
                    tbuf[pl.ds(p * 256, 256), cols], x, NT, preferred_element_type=F32
                )
                before = sums[p][k // 2]
                sums[p][k // 2] = part if before is None else before + part
        swapped = jnp.where(row4 < 2, pltpu.roll(sums[1][1], 254, 0), -pltpu.roll(sums[1][1], 2, 0))
        for p, second in ((0, sums[0][1]), (1, swapped)):
            first = sums[p][0].reshape(8, 2, 16, HALF)
            second = second.reshape(8, 2, 16, HALF)
            even, odd = first[:, 0] + second[:, 0], first[:, 1] - second[:, 1]
            both = jnp.stack([even, odd], axis=1).astype(BF16).reshape(2, 8, 16, HALF)
            for c in range(2):
                send1[c, pl.ds(h * 16 + p * 8, 8)] = both[c]
        if h == 0:
            for copy in constants:
                copy.start()
            pl.semaphore_wait(barrier, 67)
        for c in range(2):
            for dz, dy in FAR_FIRST:
                to, slot = zy_partner(dz, dy)
                pltpu.make_async_remote_copy(
                    send1.at[c, h * 16 + slot], recv1.at[c, h * 16 + mine1], ssem.at[c], rsem.at[c],
                    device_id=(to, col), device_id_type=MESH,
                ).start()

            recv1[c, h * 16 + mine1] = send1[c, h * 16 + mine1]

    constants[2].wait()
    left = lax.broadcasted_iota(jnp.int32, (GROUP, 128), 1) < 64

    @pl.loop(0, 64)
    def _(i):
        wr, wi = wbuf[0, i].astype(F32), wbuf[1, i].astype(F32)
        wr2, wi2 = pltpu.roll(wr, 64, 1), pltpu.roll(wi, 64, 1)
        wmix[0, 0, i] = jnp.where(left, wr, wr2)
        wmix[0, 1, i] = jnp.where(left, -wi, wi2)
        wmix[1, 0, i] = jnp.where(left, wr2, wr)
        wmix[1, 1, i] = jnp.where(left, -wi2, wi)

    for copy in constants[3:5]:
        copy.wait()
    lane_c = lax.broadcasted_iota(jnp.int32, (GROUP, HALF), 1) % GROUP
    row_c = lax.broadcasted_iota(jnp.int32, (GROUP, HALF), 0)
    pick = jnp.where(lane_c == row_c, 1.0, 0.0).astype(BF16)

    mine2 = col * 4 + xlo * 2 + core
    for c in range(2):
        wait_bytes(recv1.at[c, pl.ds(0, 30)], rsem.at[c])
        total = [None] * 2
        for h in range(2):
            lanes = pl.ds(h * HALF, HALF)
            data = recv1[c, pl.ds(h * 16, 16)].reshape(256, HALF)
            cosine, sine = ftw_v[0, :, lanes], ftw_v[1, :, lanes]
            for two in range(2):
                part = jnp.dot(fxt_v[pl.ds(two * 256, 256), :], data, preferred_element_type=F32)
                part = part.reshape(2, 2, 2, KX, HALF)
                real, imag = part[:, 0], part[:, 1]
                turned = jnp.stack([
                    real * cosine + imag * sine,
                    imag * cosine - real * sine,
                ], axis=1).reshape(256, HALF).astype(BF16)
                summed = lax.dot_general(pick, turned, NT, preferred_element_type=F32)
                total[two] = summed if h == 0 else total[two] + summed
        for two in range(2):
            for block in range(2):
                send2[c, two * 2 + block] = total[two][:, block * 128:(block + 1) * 128].astype(BF16)

        for k in (4, 6, 5, 7, 1, 3, 2):
            to, col2, block = near_partner(k)
            pltpu.make_async_remote_copy(
                send2.at[c, block], recv2.at[c, mine2], ssem.at[2 + c], rsem.at[2 + c],
                device_id=(to, col2), device_id_type=MESH,
            ).start()

        recv2[c, mine2] = send2[c, xlo * 2 + core]

    for copy in constants[5:7]:
        copy.wait()
    mine3 = (y % 2) * 32 + (z * 2 + y // 2) * 4 + xlo * 2 + core
    for c in range(2):
        wait_bytes(recv2.at[c, pl.ds(0, 7)], rsem.at[2 + c])
        for half in range(2):
            sum4 = recv2[c, half * 4].astype(F32)
            for k in range(1, 4):
                sum4 += recv2[c, half * 4 + k].astype(F32)
            sum4 = sum4.astype(BF16).astype(F32)
            modes[0, pl.ds(half * GROUP, GROUP), :] = sum4
            modes[1, pl.ds(half * GROUP, GROUP), :] = pltpu.roll(sum4, 64, 1)

        def mix(step, mixed):
            rows = pl.ds(pl.multiple_of(step * 8, 8), 8)
            straight, crossed = modes[0, rows, :], modes[1, rows, :]
            for k in range(8):
                i = step * 8 + k
                mixed += wmix[c, 0, i] * straight[k:k + 1] + wmix[c, 1, i] * crossed[k:k + 1]
            return mixed

        mixed = lax.fori_loop(0, 8, mix, jnp.zeros((GROUP, 128), F32)).astype(BF16)
        spread = lax.dot_general(mixed, pick[:, 0:128], TN, preferred_element_type=F32)
        other = jnp.minimum(core + c, 1)
        cosine, sine = itw_v[other, 0], itw_v[other, 1]
        real, imag = spread[0:64], spread[64:128]
        turned = jnp.concatenate([
            real * cosine - imag * sine,
            real * sine + imag * cosine,
        ]).astype(BF16)
        for q in range(4):
            rows = jnp.dot(ixt_v[pl.ds(q * 256, 256), :], turned, preferred_element_type=F32)
            send3[c, pl.ds(q * 16, 16)] = rows.astype(BF16).reshape(16, 16, 128)

        def share(k):
            dz, dy = 2 + 3 * (k // 16), 2 + 3 * ((k // 4) % 4)
            dx, dcore = 1 - (k // 2) % 2, 1 - k % 2
            z2, y2, xlo2, core2 = (z + dz) % 4, (y + dy) % 4, (xlo + dx) % 2, (core + dcore) % 2
            to = z2 * 16 + xlo2 * 8 + y2 * 2 + core2
            pltpu.make_async_remote_copy(
                send3.at[c, to], recv3.at[c, mine3], ssem.at[4 + c], rsem.at[4 + c],
                device_id=(to, col), device_id_type=MESH,
            ).start()

        pl.loop(0, 43)(share)
        pl.loop(44, 64)(share)
        recv3[c, mine3] = send3[c, g]

    for copy in constants[:2] + constants[7:]:
        copy.wait()
    square = (GROUP, GROUP)
    diagonal = lax.broadcasted_iota(jnp.int32, square, 0) == lax.broadcasted_iota(jnp.int32, square, 1)

    def column(row):
        part = 0.5 * jnp.sum(jnp.where(diagonal, row, 0.0), axis=1, keepdims=True)
        return jnp.broadcast_to(part, (GROUP, PRE))

    gain_c, bias_c = column(gain_v[...]), column(bias_v[...])

    @pl.loop(0, XDEV)
    def _(x):
        rows = pl.ds(pl.multiple_of(x * GROUP, GROUP), GROUP)
        for at in range(0, PLANE, PRE):
            pre[rows, pl.ds(at, PRE)] = xbuf[rows, pl.ds(at, PRE)].astype(F32) * gain_c + bias_c

    for c in range(2):
        wait_bytes(send1.at[c, pl.ds(0, 30)], ssem.at[c])
        wait_bytes(recv2.at[c, pl.ds(0, 7)], ssem.at[2 + c])
    for c in range(2):
        wait_bytes(recv3.at[c, pl.ds(0, 63)], rsem.at[4 + c])
        out[c] = recv3[c]
    for c in range(2):
        wait_bytes(send3.at[c, pl.ds(0, 63)], ssem.at[4 + c])


def finish_kernel(slabs, pre, table, out, vals, obuf, evens, odds, osem):
    c1 = 2.0 * math.sqrt(2.0 / math.pi)
    c3 = 8.0 * 0.044715 * math.sqrt(2.0 / math.pi)

    def store(j):
        return [
            pltpu.make_async_copy(
                obuf.at[j % 2, s], out.at[:, pl.ds(s * FOLD + j * STEP, STEP)], osem.at[j % 2, s]
            )
            for s in range(2)
        ]

    def products(n):
        cols = pl.ds(n * BLOCK, BLOCK)
        evens[n % 2] = jnp.dot(vals[:, 0:256], table[0:256, cols], preferred_element_type=F32)
        odds[n % 2] = jnp.dot(vals[:, 256:512], table[256:512, cols], preferred_element_type=F32)

    upper = lax.broadcasted_iota(jnp.int32, (32, 8, 128), 1) < 4
    for c in range(2):
        for pair in range(2):
            both = slabs[c].astype(F32)[:, pair * 8:(pair + 1) * 8, :].reshape(32, 2, 8, 128)
            first, second = both[:, 0], both[:, 1]
            quarters = (
                jnp.where(upper, first, pltpu.roll(second, 4, 1)),
                jnp.where(upper, pltpu.roll(first, 4, 1), second),
            )
            for q in range(2):
                quarter = quarters[q].reshape(256, 128)
                rows = pl.ds((pair * 2 + q) * 128, 128)
                for p in range(2):
                    vals[rows, pl.ds(p * 256 + c * 128, 128)] = quarter[p * 128:(p + 1) * 128].T.astype(BF16)
    products(0)
    steps = FOLD // STEP
    for j in range(steps):
        if j >= 2:
            for copy in store(j - 2):
                copy.wait()
        for i in range(STEP // BLOCK):
            n = j * (STEP // BLOCK) + i
            if (n + 1) * BLOCK < FOLD:
                products(n + 1)
            for m in range(ROWS // MB):
                rows = pl.ds(m * MB, MB)
                even, odd = evens[n % 2, rows, :], odds[n % 2, rows, :]
                for s in range(2):
                    spectral = even + odd if s == 0 else even - odd
                    v = spectral + pre[rows, pl.ds(s * FOLD + n * BLOCK, BLOCK)]
                    u = v * (c1 + c3 * (v * v))
                    obuf[j % 2, s, rows, pl.ds(i * BLOCK, BLOCK)] = (v + v * jnp.tanh(u)).astype(BF16)
        for copy in store(j):
            copy.start()
    for j in (steps - 2, steps - 1):
        for copy in store(j):
            copy.wait()


def in_hbm(array):
    return pltpu.with_memory_space_constraint(array, pltpu.HBM)


def shards(state_field, spectral_weight, local_weight, channel_bias):
    anywhere = pl.BlockSpec(memory_space=pltpu.HBM)
    vmem = pl.BlockSpec(memory_space=pltpu.VMEM)
    slabs, pre, table_v = pl.pallas_call(
        exchange_kernel,
        out_shape=[
            jax.ShapeDtypeStruct((2, 64, 16, 128), BF16),
            jax.ShapeDtypeStruct((ROWS, PLANE), F32),
            jax.ShapeDtypeStruct((512, FOLD), BF16),
        ],
        in_specs=[anywhere] * 9,
        out_specs=[vmem] * 3,
        scratch_shapes=[
            pltpu.VMEM((ROWS, PLANE), BF16),
            pltpu.VMEM((2, 64, GROUP, 128), BF16),
            pltpu.VMEM((1, GROUP), F32),
            pltpu.VMEM((1, GROUP), F32),
            pltpu.VMEM((512, 256), BF16),
            pltpu.VMEM((2, KX, ROWS), F32),
            pltpu.VMEM((1024, 128), BF16),
            pltpu.VMEM((2, 2, 64, 128), F32),
            pltpu.VMEM((2, 2, 64, GROUP, 128), F32),
            pltpu.VMEM((2, 32, 16, HALF), BF16),
            pltpu.VMEM((2, 32, 16, HALF), BF16),
            pltpu.VMEM((2, 4, GROUP, 128), BF16),
            pltpu.VMEM((2, 8, GROUP, 128), BF16),
            pltpu.VMEM((2, 64, 128), F32),
            pltpu.VMEM((2, 64, 16, 128), BF16),
            pltpu.VMEM((2, 64, 16, 128), BF16),
            pltpu.SemaphoreType.DMA((3,)),
            pltpu.SemaphoreType.DMA((4 * PIECES,)),
            pltpu.SemaphoreType.DMA((7,)),
            pltpu.SemaphoreType.DMA((6,)),
            pltpu.SemaphoreType.DMA((6,)),
        ],
        compiler_params=pltpu.CompilerParams(
            collective_id=0, has_side_effects=True, vmem_limit_bytes=24 << 20
        ),
        name="exchange",
    )(
        in_hbm(state_field.reshape(ROWS, PLANE)),
        in_hbm(spectral_weight),
        in_hbm(local_weight.reshape(1, GROUP)),
        in_hbm(channel_bias.reshape(1, GROUP)),
        *[in_hbm(jnp.asarray(make())) for make in (
            plane_table, forward_x_table, forward_twiddle, inverse_x_table, inverse_twiddle
        )],
    )
    result = pl.pallas_call(
        finish_kernel,
        out_shape=jax.ShapeDtypeStruct((ROWS, PLANE), BF16),
        in_specs=[vmem] * 3,
        out_specs=anywhere,
        scratch_shapes=[
            pltpu.VMEM((ROWS, 512), BF16),
            pltpu.VMEM((2, 2, ROWS, STEP), BF16),
            pltpu.VMEM((2, ROWS, BLOCK), F32),
            pltpu.VMEM((2, ROWS, BLOCK), F32),
            pltpu.SemaphoreType.DMA((2, 2)),
        ],
        compiler_params=pltpu.CompilerParams(vmem_limit_bytes=16 << 20),
        name="finish",
    )(slabs, pre, table_v)
    return result.reshape(state_field.shape)


def solution(mesh):
    return jax.shard_map(
        shards,
        mesh=mesh,
        in_specs=(P("gx", "col", None), P(None, None, "col", "gx"), P("col"), P("col")),
        out_specs=P("gx", "col", None),
        check_vma=False,
    )
```

```python
import math

import jax
import jax.numpy as jnp
import ml_dtypes
import numpy as np
from jax import lax
from jax.experimental import pallas as pl
from jax.experimental.pallas import tpu as pltpu
from jax.sharding import PartitionSpec as P

MESH = pl.DeviceIdType.MESH
BF16 = jnp.bfloat16
F32 = jnp.float32

XCELLS = 1024
YCELLS = 128
TSTEPS = 64
KX = 32
KY = 32
PLANE = YCELLS * TSTEPS
FOLD = PLANE // 2
QUARTER = PLANE // 4
XDEV = 16
GROUP = 32
ROWS = XDEV * GROUP
HALF = ROWS // 2
PIECES = 4
PIECE = FOLD // PIECES
STEP = 512
BLOCK = 256
MB = 64
PRE = 256

NT = (((1,), (1,)), ((), ()))
TN = (((0,), (0,)), ((), ()))


FAR_FIRST = sorted(
    [(dz, dy) for dz in range(4) for dy in range(4) if dz or dy],
    key=lambda o: -(min(o[0], 4 - o[0]) + min(o[1], 4 - o[1])),
)


def freq(index, number):
    return np.where(index < number // 2, index, index - number)


def plane_table():
    p, z, yh, c, xlo, half, r, kt2 = np.meshgrid(
        *[np.arange(n) for n in (2, 4, 2, 2, 2, 2, 2, 2)], indexing="ij"
    )
    ky = freq((z * 8 + xlo * 4 + yh * 2 + p).reshape(-1), KY)
    kt = (half * 4 + c * 2 + kt2).reshape(-1)
    r = r.reshape(-1)
    cells = np.arange(FOLD)
    y, t = cells // TSTEPS, cells % TSTEPS
    phase = (ky[:, None] * y[None] * TSTEPS + kt[:, None] * t[None] * YCELLS) % PLANE
    angle = phase * (2.0 * math.pi / PLANE)
    table = np.where(r[:, None] == 0, np.cos(angle), -np.sin(angle))
    return table.astype(ml_dtypes.bfloat16)


def forward_x_table():
    kx = freq(np.arange(KX), KX)
    slot = np.arange(16)
    p, z, yh = slot // 8, (slot // 2) % 4, slot % 2
    angle = 2.0 * math.pi * ((kx[:, None] * (8 * z + yh * 2 + p)[None]) % 32) / 32
    cosine, sine = np.cos(angle), np.sin(angle)
    table = np.zeros((4, 2, 2, KX, 16, 4, 2, 2))
    for block in range(4):
        for k in range(2):
            table[block, 0, k, :, :, block, 0, k] = cosine
            table[block, 0, k, :, :, block, 1, k] = sine
            table[block, 1, k, :, :, block, 1, k] = cosine
            table[block, 1, k, :, :, block, 0, k] = -sine
    return table.reshape(512, 256).astype(ml_dtypes.bfloat16)


def forward_twiddle():
    kx = freq(np.arange(KX), KX)
    scale = 1.0 / math.sqrt(XCELLS * PLANE)
    place = np.arange(4)
    offset = (place // 2) * 128 + (place % 2) * 16
    lanes = np.arange(ROWS) // GROUP
    angle = 2.0 * math.pi * ((kx[None, :, None] * (offset[:, None, None] + lanes)) % XCELLS) / XCELLS
    return (np.stack([np.cos(angle), np.sin(angle)], axis=1) * scale).astype(np.float32)


def inverse_x_table():
    kx = freq(np.arange(KX), KX)
    start = np.arange(2)[:, None] * 8 + np.arange(32)[None] * 32
    angle = 2.0 * math.pi * ((kx * start[..., None]) % XCELLS) / XCELLS
    cosine, sine = np.cos(angle), np.sin(angle)
    table = np.zeros((2, 32, 2, 2, 2, 2, 2, 2, KX))
    for core in range(2):
        for k in range(2):
            table[:, :, core, 0, k, core, 0, k] = cosine
            table[:, :, core, 0, k, core, 1, k] = -sine
            table[:, :, core, 1, k, core, 0, k] = sine
            table[:, :, core, 1, k, core, 1, k] = cosine
    return table.reshape(2, 256, 256).astype(ml_dtypes.bfloat16)


def inverse_twiddle():
    kx = np.tile(freq(np.arange(KX), KX), 2)
    kt2 = np.repeat(np.arange(2), KX)
    lanes = np.arange(2)[:, None] * XDEV + np.arange(HALF)[None] // GROUP
    angle = 2.0 * math.pi * ((kx[None, :, None] * lanes[:, None]) % XCELLS) / XCELLS
    parts = np.stack([np.cos(angle), np.sin(angle)], axis=1)
    weight = np.stack([np.where(kt2 + 2 * other == 0, 1.0, 2.0) for other in range(2)])
    scale = 0.5 / math.sqrt(PLANE)
    return (parts[:, None] * weight[None, :, None, :, None] * scale).astype(np.float32)


def place_of(g):
    return g // 16, (g // 8) % 2, (g // 2) % 4, g % 2


def arrange(shares, vals):
    tiles = shares.astype(F32).reshape(16, 2, 2, 8, HALF)
    tiles = jnp.stack([tiles[:, 0, 0], tiles[:, 1, 0], tiles[:, 0, 1], tiles[:, 1, 1]], axis=1)
    vals[...] = tiles.reshape(512, HALF).T.astype(BF16)


def transform_back(vals, pre, table, evens, odds, put, after):
    c1 = 2.0 * math.sqrt(2.0 / math.pi)
    c3 = 8.0 * 0.044715 * math.sqrt(2.0 / math.pi)

    def products(n):
        cols = pl.ds(n * BLOCK, BLOCK)
        evens[n % 2] = jnp.dot(vals[:, 0:256], table[0:256, cols], preferred_element_type=F32)
        odds[n % 2] = jnp.dot(vals[:, 256:512], table[256:512, cols], preferred_element_type=F32)

    products(0)
    for n in range(FOLD // BLOCK):
        if (n + 1) * BLOCK < FOLD:
            products(n + 1)
        for m in range(HALF // MB):
            rows = pl.ds(m * MB, MB)
            even, odd = evens[n % 2, rows, :], odds[n % 2, rows, :]
            for s in range(2):
                spectral = even + odd if s == 0 else even - odd
                v = spectral + pre[rows, pl.ds(s * FOLD + n * BLOCK, BLOCK)]
                u = v * (c1 + c3 * (v * v))
                put(n, s, rows, (v + v * jnp.tanh(u)).astype(BF16))
        after(n)


def exchange_kernel(
    state, weight, gain, bias, table, fxt, ftw, ixt, itw, out, shares, pre1, tbuf,
    xbuf, wbuf, gain_v, bias_v, fxt_v, ftw_v, ixt_v, itw_v, wmix,
    send1, recv1, send2, recv2, modes, own, near, turned_v, send3, recv3,
    pre0, vals, evens, odds,
    tsem, xsem, csem, ssem, rsem,
):
    g = lax.axis_index("gx")
    col = lax.axis_index("col")
    z, xlo, y, core = place_of(g)

    def zy_partner(dz, dy):
        z2, y2 = (z + dz) % 4, (y + dy) % 4
        return z2 * 16 + xlo * 8 + y2 * 2 + core, (y2 % 2) * 8 + z2 * 2 + y2 // 2

    def near_partner(k):
        xlo2, core2, col2 = (xlo + k % 2) % 2, (core + (k // 2) % 2) % 2, (col + k // 4) % 2
        return z * 16 + xlo2 * 8 + y * 2 + core2, col2, xlo2 * 2 + core2

    def wait_bytes(ref, sem):
        pltpu.make_async_copy(ref, ref, sem).wait()

    table_loads = []
    for k in range(2):
        cols = pl.ds(k * PIECE, PIECE)
        table_loads.append(pltpu.make_async_copy(table.at[:, cols], tbuf.at[:, cols], tsem.at[k]))
    rest = pl.ds(QUARTER, QUARTER)
    table_loads.append(pltpu.make_async_copy(table.at[:, rest], tbuf.at[:, rest], tsem.at[2]))
    state_loads = {}
    for h in range(2):
        for k in range(PIECES):
            for s in range(2):
                rows, at = pl.ds(h * HALF, HALF), pl.ds(s * FOLD + k * PIECE, PIECE)
                state_loads[h, k, s] = pltpu.make_async_copy(
                    state.at[rows, at], xbuf.at[rows, at], xsem.at[(h * PIECES + k) * 2 + s]
                )
    for k in range(PIECES):
        if k < 2:
            table_loads[k].start()
        for s in range(2):
            state_loads[0, k, s].start()
    constants = [
        pltpu.make_async_copy(gain, gain_v, csem.at[0]),
        pltpu.make_async_copy(bias, bias_v, csem.at[1]),
        pltpu.make_async_copy(weight, wbuf, csem.at[2]),
        pltpu.make_async_copy(fxt, fxt_v, csem.at[3]),
        pltpu.make_async_copy(ftw.at[xlo * 2 + core], ftw_v, csem.at[4]),
        pltpu.make_async_copy(itw.at[core], itw_v, csem.at[5]),
        pltpu.make_async_copy(ixt, ixt_v, csem.at[6]),
        table_loads[2],
    ]

    barrier = pltpu.get_barrier_semaphore()

    @pl.loop(1, 64)
    def _(k):
        pl.semaphore_signal(barrier, inc=1, device_id=((g + k) % 64, col), device_id_type=MESH)

    @pl.loop(4, 8)
    def _(k):
        to, col2, _slot = near_partner(k)
        pl.semaphore_signal(barrier, inc=1, device_id=(to, col2), device_id_type=MESH)

    row4 = lax.broadcasted_iota(jnp.int32, (256, HALF), 0) % 4
    mine1 = (y % 2) * 8 + z * 2 + y // 2
    for h in range(2):
        rows = pl.ds(h * HALF, HALF)
        sums = [[None, None], [None, None]]
        for k in range(PIECES):
            lo = pl.ds(k * PIECE, PIECE)
            hi = pl.ds(FOLD + k * PIECE, PIECE)
            cols = pl.ds((k % 2) * PIECE, PIECE)
            if h == 0 and k < 2:
                table_loads[k].wait()
            for s in range(2):
                state_loads[h, k, s].wait()
                if h == 0:
                    state_loads[1, k, s].start()
            x0, x1 = xbuf[rows, lo], xbuf[rows, hi]
            for p, x in ((0, x0 + x1), (1, x0 - x1)):
                part = lax.dot_general(
                    tbuf[pl.ds(p * 256, 256), cols], x, NT, preferred_element_type=F32
                )
                before = sums[p][k // 2]
                sums[p][k // 2] = part if before is None else before + part
        swapped = jnp.where(row4 < 2, pltpu.roll(sums[1][1], 254, 0), -pltpu.roll(sums[1][1], 2, 0))
        for p, second in ((0, sums[0][1]), (1, swapped)):
            first = sums[p][0].reshape(4, 2, 32, HALF)
            second = second.reshape(4, 2, 32, HALF)
            even, odd = first[:, 0] + second[:, 0], first[:, 1] - second[:, 1]
            both = jnp.stack([even, odd], axis=1).astype(BF16).reshape(8, 2, 16, HALF)
            for c in range(2):
                send1[c, pl.ds(h * 16 + p * 8, 8)] = both[:, c]
        if h == 0:
            for copy in constants:
                copy.start()
            pl.semaphore_wait(barrier, 67)
        for c in range(2):
            for dz, dy in FAR_FIRST:
                to, slot = zy_partner(dz, dy)
                pltpu.make_async_remote_copy(
                    send1.at[c, h * 16 + slot], recv1.at[c, h * 16 + mine1], ssem.at[c], rsem.at[c],
                    device_id=(to, col), device_id_type=MESH,
                ).start()

            recv1[c, h * 16 + mine1] = send1[c, h * 16 + mine1]

    constants[2].wait()
    left = lax.broadcasted_iota(jnp.int32, (GROUP, 128), 1) < 64

    @pl.loop(0, 64)
    def _(i):
        wr, wi = wbuf[0, i].astype(F32), wbuf[1, i].astype(F32)
        wr2, wi2 = pltpu.roll(wr, 64, 1), pltpu.roll(wi, 64, 1)
        wmix[0, 0, i] = jnp.where(left, wr, wr2)
        wmix[0, 1, i] = jnp.where(left, -wi, wi2)
        wmix[1, 0, i] = jnp.where(left, wr2, wr)
        wmix[1, 1, i] = jnp.where(left, -wi2, wi)

    for copy in constants[3:5]:
        copy.wait()
    lane_c = lax.broadcasted_iota(jnp.int32, (GROUP, HALF), 1) % GROUP
    row_c = lax.broadcasted_iota(jnp.int32, (GROUP, HALF), 0)
    pick = jnp.where(lane_c == row_c, 1.0, 0.0).astype(BF16)

    mine2 = col * 4 + xlo * 2 + core
    for c in range(2):
        wait_bytes(recv1.at[c, pl.ds(0, 30)], rsem.at[c])
        total = [None] * 2
        for h in range(2):
            lanes = pl.ds(h * HALF, HALF)
            data = recv1[c, pl.ds(h * 16, 16)].reshape(256, HALF)
            cosine, sine = ftw_v[0, :, lanes], ftw_v[1, :, lanes]
            for two in range(2):
                part = jnp.dot(fxt_v[pl.ds(two * 256, 256), :], data, preferred_element_type=F32)
                part = part.reshape(2, 2, 2, KX, HALF)
                real, imag = part[:, 0], part[:, 1]
                turned = jnp.stack([
                    real * cosine + imag * sine,
                    imag * cosine - real * sine,
                ], axis=1).reshape(256, HALF).astype(BF16)
                summed = lax.dot_general(pick, turned, NT, preferred_element_type=F32)
                total[two] = summed if h == 0 else total[two] + summed
        for two in range(2):
            for block in range(2):
                send2[c, two * 2 + block] = total[two][:, block * 128:(block + 1) * 128].astype(BF16)

        for k in (4, 6, 5, 7, 1, 3, 2):
            to, col2, block = near_partner(k)
            pltpu.make_async_remote_copy(
                send2.at[c, block], recv2.at[c, mine2], ssem.at[2 + c], rsem.at[2 + c],
                device_id=(to, col2), device_id_type=MESH,
            ).start()

        recv2[c, mine2] = send2[c, xlo * 2 + core]

    for copy in constants[5:7]:
        copy.wait()

    def turn(mixed, of, c):
        spread = lax.dot_general(mixed, pick, TN, preferred_element_type=F32)
        other = jnp.minimum(of + c, 1)
        cosine, sine = itw_v[other, 0], itw_v[other, 1]
        real, imag = spread[0:64], spread[64:128]
        turned_v[c, of] = jnp.concatenate([
            real * cosine - imag * sine,
            real * sine + imag * cosine,
        ]).astype(BF16)

    for c in range(2):
        wait_bytes(recv2.at[c, pl.ds(0, 7)], rsem.at[2 + c])
        for half in range(2):
            sum4 = recv2[c, half * 4].astype(F32)
            for k in range(1, 4):
                sum4 += recv2[c, half * 4 + k].astype(F32)
            sum4 = sum4.astype(BF16).astype(F32)
            modes[0, pl.ds(half * GROUP, GROUP), :] = sum4
            modes[1, pl.ds(half * GROUP, GROUP), :] = pltpu.roll(sum4, 64, 1)

        def mix(step, mixed):
            rows = pl.ds(pl.multiple_of(step * 8, 8), 8)
            straight, crossed = modes[0, rows, :], modes[1, rows, :]
            for k in range(8):
                i = step * 8 + k
                mixed += wmix[c, 0, i] * straight[k:k + 1] + wmix[c, 1, i] * crossed[k:k + 1]
            return mixed

        own[c] = lax.fori_loop(0, 8, mix, jnp.zeros((GROUP, 128), F32)).astype(BF16)
        pltpu.make_async_remote_copy(
            own.at[c], near.at[c], ssem.at[4 + c], rsem.at[4 + c],
            device_id=(g + 1 - 2 * core, col), device_id_type=MESH,
        ).start()
        turn(own[c], core, c)
    for c in range(2):
        wait_bytes(near.at[c], rsem.at[4 + c])
        turn(near[c], 1 - core, c)

    chip = z * 8 + xlo * 4 + y
    mine3 = (y % 2) * 16 + z * 4 + (y // 2) * 2 + xlo
    for half in range(2):
        tiles = [
            jnp.dot(ixt_v[half], turned_v[c].reshape(256, HALF), preferred_element_type=F32).reshape(32, 8, HALF)
            for c in range(2)
        ]
        send3[half] = jnp.concatenate(tiles, axis=1).astype(BF16)

        def share(k):
            z2, y2 = (z + 2 + 3 * (k // 8)) % 4, (y + 2 + 3 * ((k // 2) % 4)) % 4
            to = z2 * 8 + ((xlo + 1 - k % 2) % 2) * 4 + y2
            pltpu.make_async_remote_copy(
                send3.at[half, to], recv3.at[half, mine3], ssem.at[6 + half], rsem.at[6 + half],
                device_id=(to * 2 + core, col), device_id_type=MESH,
            ).start()

        pl.loop(0, 21)(share)
        pl.loop(22, 32)(share)
        recv3[half, mine3] = send3[half, chip]

    for copy in constants[:2] + constants[7:]:
        copy.wait()
    square = (GROUP, GROUP)
    diagonal = lax.broadcasted_iota(jnp.int32, square, 0) == lax.broadcasted_iota(jnp.int32, square, 1)

    def column(row):
        part = 0.5 * jnp.sum(jnp.where(diagonal, row, 0.0), axis=1, keepdims=True)
        return jnp.broadcast_to(part, (GROUP, PRE))

    gain_c, bias_c = column(gain_v[...]), column(bias_v[...])

    for half, pre in ((0, pre0), (1, pre1)):
        @pl.loop(0, XDEV // 2)
        def _(x):
            start = pl.multiple_of(x * GROUP, GROUP)
            for at in range(0, PLANE, PRE):
                cells = xbuf[pl.ds(start + half * HALF, GROUP), pl.ds(at, PRE)].astype(F32)
                pre[pl.ds(start, GROUP), pl.ds(at, PRE)] = cells * gain_c + bias_c

    for c in range(2):
        wait_bytes(send1.at[c, pl.ds(0, 30)], ssem.at[c])
        wait_bytes(recv2.at[c, pl.ds(0, 7)], ssem.at[2 + c])
        wait_bytes(own.at[c], ssem.at[4 + c])

    def put(n, s, rows, values):
        out[rows, pl.ds(s * FOLD + n * BLOCK, BLOCK)] = values

    wait_bytes(recv3.at[0, pl.ds(0, 31)], rsem.at[6])
    arrange(recv3[0], vals)
    transform_back(vals, pre0, tbuf, evens, odds, put, lambda n: None)
    wait_bytes(recv3.at[1, pl.ds(0, 31)], rsem.at[7])
    shares[...] = recv3[1]
    for half in range(2):
        wait_bytes(send3.at[half, pl.ds(0, 31)], ssem.at[6 + half])


def finish_kernel(first, shares, pre, table, out, vals, obuf, evens, odds, fsem, osem):
    per = STEP // BLOCK

    def store(j, s):
        cols = pl.ds(s * FOLD + j * STEP, STEP)
        return pltpu.make_async_copy(obuf.at[:, cols], out.at[pl.ds(HALF, HALF), cols], osem.at[j, s])

    def put(n, s, rows, values):
        obuf[rows, pl.ds(s * FOLD + n * BLOCK, BLOCK)] = values

    def after(n):
        if n % per == per - 1:
            store(n // per, 0).start()
            store(n // per, 1).start()

    first_half = pltpu.make_async_copy(first, out.at[pl.ds(0, HALF), :], fsem)
    first_half.start()
    arrange(shares[...], vals)
    transform_back(vals, pre, table, evens, odds, put, after)
    for j in range(FOLD // STEP):
        store(j, 0).wait()
        store(j, 1).wait()
    first_half.wait()


def in_hbm(array):
    return pltpu.with_memory_space_constraint(array, pltpu.HBM)


def shards(state_field, spectral_weight, local_weight, channel_bias):
    anywhere = pl.BlockSpec(memory_space=pltpu.HBM)
    vmem = pl.BlockSpec(memory_space=pltpu.VMEM)
    first, shares, pre, table_v = pl.pallas_call(
        exchange_kernel,
        out_shape=[
            jax.ShapeDtypeStruct((HALF, PLANE), BF16),
            jax.ShapeDtypeStruct((32, 16, HALF), BF16),
            jax.ShapeDtypeStruct((HALF, PLANE), F32),
            jax.ShapeDtypeStruct((512, FOLD), BF16),
        ],
        in_specs=[anywhere] * 9,
        out_specs=[vmem] * 4,
        scratch_shapes=[
            pltpu.VMEM((ROWS, PLANE), BF16),
            pltpu.VMEM((2, 64, GROUP, 128), BF16),
            pltpu.VMEM((1, GROUP), F32),
            pltpu.VMEM((1, GROUP), F32),
            pltpu.VMEM((512, 256), BF16),
            pltpu.VMEM((2, KX, ROWS), F32),
            pltpu.VMEM((2, 256, 256), BF16),
            pltpu.VMEM((2, 2, 64, HALF), F32),
            pltpu.VMEM((2, 2, 64, GROUP, 128), F32),
            pltpu.VMEM((2, 32, 16, HALF), BF16),
            pltpu.VMEM((2, 32, 16, HALF), BF16),
            pltpu.VMEM((2, 4, GROUP, 128), BF16),
            pltpu.VMEM((2, 8, GROUP, 128), BF16),
            pltpu.VMEM((2, 64, 128), F32),
            pltpu.VMEM((2, GROUP, 128), BF16),
            pltpu.VMEM((2, GROUP, 128), BF16),
            pltpu.VMEM((2, 2, 128, HALF), BF16),
            pltpu.VMEM((2, 32, 16, HALF), BF16),
            pltpu.VMEM((2, 32, 16, HALF), BF16),
            pltpu.VMEM((HALF, PLANE), F32),
            pltpu.VMEM((HALF, 512), BF16),
            pltpu.VMEM((2, HALF, BLOCK), F32),
            pltpu.VMEM((2, HALF, BLOCK), F32),
            pltpu.SemaphoreType.DMA((3,)),
            pltpu.SemaphoreType.DMA((4 * PIECES,)),
            pltpu.SemaphoreType.DMA((7,)),
            pltpu.SemaphoreType.DMA((8,)),
            pltpu.SemaphoreType.DMA((8,)),
        ],
        compiler_params=pltpu.CompilerParams(
            collective_id=0, has_side_effects=True, vmem_limit_bytes=32 << 20
        ),
        name="exchange",
    )(
        in_hbm(state_field.reshape(ROWS, PLANE)),
        in_hbm(spectral_weight),
        in_hbm(local_weight.reshape(1, GROUP)),
        in_hbm(channel_bias.reshape(1, GROUP)),
        *[in_hbm(jnp.asarray(make())) for make in (
            plane_table, forward_x_table, forward_twiddle, inverse_x_table, inverse_twiddle
        )],
    )
    result = pl.pallas_call(
        finish_kernel,
        out_shape=jax.ShapeDtypeStruct((ROWS, PLANE), BF16),
        in_specs=[vmem] * 4,
        out_specs=anywhere,
        scratch_shapes=[
            pltpu.VMEM((HALF, 512), BF16),
            pltpu.VMEM((HALF, PLANE), BF16),
            pltpu.VMEM((2, HALF, BLOCK), F32),
            pltpu.VMEM((2, HALF, BLOCK), F32),
            pltpu.SemaphoreType.DMA,
            pltpu.SemaphoreType.DMA((FOLD // STEP, 2)),
        ],
        compiler_params=pltpu.CompilerParams(vmem_limit_bytes=16 << 20),
        name="finish",
    )(first, shares, pre, table_v)
    return result.reshape(state_field.shape)


def solution(mesh):
    return jax.shard_map(
        shards,
        mesh=mesh,
        in_specs=(P("gx", "col", None), P(None, None, "col", "gx"), P("col"), P("col")),
        out_specs=P("gx", "col", None),
        check_vma=False,
    )
```

```python
import math

import jax
import jax.numpy as jnp
import ml_dtypes
import numpy as np
from jax import lax
from jax.experimental import pallas as pl
from jax.experimental.pallas import tpu as pltpu
from jax.sharding import PartitionSpec as P

MESH = pl.DeviceIdType.MESH
BF16 = jnp.bfloat16
F32 = jnp.float32

XCELLS = 1024
YCELLS = 128
TSTEPS = 64
KX = 32
KY = 32
PLANE = YCELLS * TSTEPS
FOLD = PLANE // 2
QUARTER = PLANE // 4
XDEV = 16
GROUP = 32
ROWS = XDEV * GROUP
HALF = ROWS // 2
PIECES = 4
PIECE = FOLD // PIECES
STEP = 512
BLOCK = 256
MB = 64
PRE = 256

NT = (((1,), (1,)), ((), ()))
TN = (((0,), (0,)), ((), ()))


FAR_FIRST = sorted(
    [(dz, dy) for dz in range(4) for dy in range(4) if dz or dy],
    key=lambda o: -(min(o[0], 4 - o[0]) + min(o[1], 4 - o[1])),
)


def freq(index, number):
    return np.where(index < number // 2, index, index - number)


def plane_table():
    p, z, yh, c, xlo, half, r, kt2 = np.meshgrid(
        *[np.arange(n) for n in (2, 4, 2, 2, 2, 2, 2, 2)], indexing="ij"
    )
    ky = freq((z * 8 + xlo * 4 + yh * 2 + p).reshape(-1), KY)
    kt = (half * 4 + c * 2 + kt2).reshape(-1)
    r = r.reshape(-1)
    cells = np.arange(FOLD)
    y, t = cells // TSTEPS, cells % TSTEPS
    phase = (ky[:, None] * y[None] * TSTEPS + kt[:, None] * t[None] * YCELLS) % PLANE
    angle = phase * (2.0 * math.pi / PLANE)
    table = np.where(r[:, None] == 0, np.cos(angle), -np.sin(angle))
    return table.astype(ml_dtypes.bfloat16)


def forward_x_table():
    kx = freq(np.arange(KX), KX)
    slot = np.arange(16)
    p, z, yh = slot // 8, (slot // 2) % 4, slot % 2
    angle = 2.0 * math.pi * ((kx[:, None] * (8 * z + yh * 2 + p)[None]) % 32) / 32
    cosine, sine = np.cos(angle), np.sin(angle)
    table = np.zeros((4, 2, 2, KX, 16, 4, 2, 2))
    for block in range(4):
        for k in range(2):
            table[block, 0, k, :, :, block, 0, k] = cosine
            table[block, 0, k, :, :, block, 1, k] = sine
            table[block, 1, k, :, :, block, 1, k] = cosine
            table[block, 1, k, :, :, block, 0, k] = -sine
    return table.reshape(512, 256).astype(ml_dtypes.bfloat16)


def forward_twiddle():
    kx = freq(np.arange(KX), KX)
    scale = 1.0 / math.sqrt(XCELLS * PLANE)
    place = np.arange(4)
    offset = (place // 2) * 128 + (place % 2) * 16
    lanes = np.arange(ROWS) // GROUP
    angle = 2.0 * math.pi * ((kx[None, :, None] * (offset[:, None, None] + lanes)) % XCELLS) / XCELLS
    return (np.stack([np.cos(angle), np.sin(angle)], axis=1) * scale).astype(np.float32)


def inverse_x_table():
    kx = freq(np.arange(KX), KX)
    start = np.arange(2)[:, None] * 8 + np.arange(32)[None] * 32
    angle = 2.0 * math.pi * ((kx * start[..., None]) % XCELLS) / XCELLS
    cosine, sine = np.cos(angle), np.sin(angle)
    table = np.zeros((2, 32, 2, 2, 2, 2, 2, 2, KX))
    for core in range(2):
        for k in range(2):
            table[:, :, core, 0, k, core, 0, k] = cosine
            table[:, :, core, 0, k, core, 1, k] = -sine
            table[:, :, core, 1, k, core, 0, k] = sine
            table[:, :, core, 1, k, core, 1, k] = cosine
    return table.reshape(2, 256, 256).astype(ml_dtypes.bfloat16)


def inverse_twiddle():
    kx = np.tile(freq(np.arange(KX), KX), 2)
    kt2 = np.repeat(np.arange(2), KX)
    lanes = np.arange(2)[:, None] * XDEV + np.arange(HALF)[None] // GROUP
    angle = 2.0 * math.pi * ((kx[None, :, None] * lanes[:, None]) % XCELLS) / XCELLS
    parts = np.stack([np.cos(angle), np.sin(angle)], axis=1)
    weight = np.stack([np.where(kt2 + 2 * other == 0, 1.0, 2.0) for other in range(2)])
    scale = 0.5 / math.sqrt(PLANE)
    return (parts[:, None] * weight[None, :, None, :, None] * scale).astype(np.float32)


def place_of(g):
    return g // 16, (g // 8) % 2, (g // 2) % 4, g % 2


def arrange(shares, vals):
    tiles = shares.astype(F32).reshape(16, 2, 2, 8, HALF)
    tiles = jnp.stack([tiles[:, 0, 0], tiles[:, 1, 0], tiles[:, 0, 1], tiles[:, 1, 1]], axis=1)
    vals[...] = tiles.reshape(512, HALF).T.astype(BF16)


def transform_back(vals, pre, table, evens, odds, put, after):
    c1 = 2.0 * math.sqrt(2.0 / math.pi)
    c3 = 8.0 * 0.044715 * math.sqrt(2.0 / math.pi)

    def products(n):
        cols = pl.ds(n * BLOCK, BLOCK)
        evens[n % 2] = jnp.dot(vals[:, 0:256], table[0:256, cols], preferred_element_type=F32)
        odds[n % 2] = jnp.dot(vals[:, 256:512], table[256:512, cols], preferred_element_type=F32)

    products(0)
    for n in range(FOLD // BLOCK):
        if (n + 1) * BLOCK < FOLD:
            products(n + 1)
        for m in range(HALF // MB):
            rows = pl.ds(m * MB, MB)
            even, odd = evens[n % 2, rows, :], odds[n % 2, rows, :]
            for s in range(2):
                spectral = even + odd if s == 0 else even - odd
                v = spectral + pre[rows, pl.ds(s * FOLD + n * BLOCK, BLOCK)]
                u = v * (c1 + c3 * (v * v))
                put(n, s, rows, (v + v * jnp.tanh(u)).astype(BF16))
        after(n)


def exchange_kernel(
    state, weight, gain, bias, table, fxt, ftw, ixt, itw, out, shares, pre1, tbuf,
    xbuf, wbuf, gain_v, bias_v, fxt_v, ftw_v, ixt_v, itw_v, wmix,
    send1, recv1, send2, recv2, modes, own, near, turned_v, send3, recv3,
    pre0, vals, evens, odds,
    tsem, xsem, csem, ssem, rsem,
):
    g = lax.axis_index("gx")
    col = lax.axis_index("col")
    z, xlo, y, core = place_of(g)

    def zy_partner(dz, dy):
        z2, y2 = (z + dz) % 4, (y + dy) % 4
        return z2 * 16 + xlo * 8 + y2 * 2 + core, (y2 % 2) * 8 + z2 * 2 + y2 // 2

    def near_partner(k):
        xlo2, core2, col2 = (xlo + k % 2) % 2, (core + (k // 2) % 2) % 2, (col + k // 4) % 2
        return z * 16 + xlo2 * 8 + y * 2 + core2, col2, xlo2 * 2 + core2

    def wait_bytes(ref, sem):
        pltpu.make_async_copy(ref, ref, sem).wait()

    table_loads = []
    for k in range(2):
        cols = pl.ds(k * PIECE, PIECE)
        table_loads.append(pltpu.make_async_copy(table.at[:, cols], tbuf.at[:, cols], tsem.at[k]))
    rest = pl.ds(QUARTER, QUARTER)
    table_loads.append(pltpu.make_async_copy(table.at[:, rest], tbuf.at[:, rest], tsem.at[2]))
    state_loads = {}
    for h in range(2):
        for k in range(PIECES):
            for s in range(2):
                rows, at = pl.ds(h * HALF, HALF), pl.ds(s * FOLD + k * PIECE, PIECE)
                state_loads[h, k, s] = pltpu.make_async_copy(
                    state.at[rows, at], xbuf.at[rows, at], xsem.at[(h * PIECES + k) * 2 + s]
                )
    for k in range(PIECES):
        if k < 2:
            table_loads[k].start()
        for s in range(2):
            state_loads[0, k, s].start()
    constants = [
        pltpu.make_async_copy(gain, gain_v, csem.at[0]),
        pltpu.make_async_copy(bias, bias_v, csem.at[1]),
        pltpu.make_async_copy(weight, wbuf, csem.at[2]),
        pltpu.make_async_copy(fxt, fxt_v, csem.at[3]),
        pltpu.make_async_copy(ftw.at[xlo * 2 + core], ftw_v, csem.at[4]),
        pltpu.make_async_copy(itw.at[core], itw_v, csem.at[5]),
        pltpu.make_async_copy(ixt, ixt_v, csem.at[6]),
        table_loads[2],
    ]

    barrier = pltpu.get_barrier_semaphore()

    @pl.loop(1, 32)
    def _(k):
        to = (g + 2 * k) % 64
        pl.semaphore_signal(barrier, inc=1, device_id=(to, col), device_id_type=MESH)

    @pl.loop(2, 8)
    def _(k):
        to, col2, _slot = near_partner(k)
        pl.semaphore_signal(barrier, inc=1, device_id=(to, col2), device_id_type=MESH)

    row4 = lax.broadcasted_iota(jnp.int32, (256, HALF), 0) % 4
    mine1 = (y % 2) * 8 + z * 2 + y // 2
    for h in range(2):
        rows = pl.ds(h * HALF, HALF)
        sums = [[None, None], [None, None]]
        for k in range(PIECES):
            lo = pl.ds(k * PIECE, PIECE)
            hi = pl.ds(FOLD + k * PIECE, PIECE)
            cols = pl.ds((k % 2) * PIECE, PIECE)
            if h == 0 and k < 2:
                table_loads[k].wait()
            for s in range(2):
                state_loads[h, k, s].wait()
                if h == 0:
                    state_loads[1, k, s].start()
            x0, x1 = xbuf[rows, lo], xbuf[rows, hi]
            for p, x in ((0, x0 + x1), (1, x0 - x1)):
                part = lax.dot_general(
                    tbuf[pl.ds(p * 256, 256), cols], x, NT, preferred_element_type=F32
                )
                before = sums[p][k // 2]
                sums[p][k // 2] = part if before is None else before + part
        swapped = jnp.where(row4 < 2, pltpu.roll(sums[1][1], 254, 0), -pltpu.roll(sums[1][1], 2, 0))
        for p, second in ((0, sums[0][1]), (1, swapped)):
            first = sums[p][0].reshape(4, 2, 32, HALF)
            second = second.reshape(4, 2, 32, HALF)
            even, odd = first[:, 0] + second[:, 0], first[:, 1] - second[:, 1]
            both = jnp.stack([even, odd], axis=1).astype(BF16).reshape(8, 2, 16, HALF)
            for c in range(2):
                send1[c, pl.ds(h * 16 + p * 8, 8)] = both[:, c]
        if h == 0:
            for copy in constants:
                copy.start()
            pl.semaphore_wait(barrier, 37)
        for c in range(2):
            for dz, dy in FAR_FIRST:
                to, slot = zy_partner(dz, dy)
                pltpu.make_async_remote_copy(
                    send1.at[c, h * 16 + slot], recv1.at[c, h * 16 + mine1], ssem.at[c], rsem.at[c],
                    device_id=(to, col), device_id_type=MESH,
                ).start()

            recv1[c, h * 16 + mine1] = send1[c, h * 16 + mine1]

    constants[2].wait()
    left = lax.broadcasted_iota(jnp.int32, (GROUP, 128), 1) < 64

    @pl.loop(0, 64)
    def _(i):
        wr, wi = wbuf[0, i].astype(F32), wbuf[1, i].astype(F32)
        wr2, wi2 = pltpu.roll(wr, 64, 1), pltpu.roll(wi, 64, 1)
        wmix[0, 0, i] = jnp.where(left, wr, wr2)
        wmix[0, 1, i] = jnp.where(left, -wi, wi2)
        wmix[1, 0, i] = jnp.where(left, wr2, wr)
        wmix[1, 1, i] = jnp.where(left, -wi2, wi)

    for copy in constants[3:5]:
        copy.wait()
    lane_c = lax.broadcasted_iota(jnp.int32, (GROUP, HALF), 1) % GROUP
    row_c = lax.broadcasted_iota(jnp.int32, (GROUP, HALF), 0)
    pick = jnp.where(lane_c == row_c, 1.0, 0.0).astype(BF16)

    mine2 = col * 4 + xlo * 2 + core
    for c in range(2):
        wait_bytes(recv1.at[c, pl.ds(0, 30)], rsem.at[c])
        total = [None] * 2
        for h in range(2):
            lanes = pl.ds(h * HALF, HALF)
            data = recv1[c, pl.ds(h * 16, 16)].reshape(256, HALF)
            cosine, sine = ftw_v[0, :, lanes], ftw_v[1, :, lanes]
            for two in range(2):
                part = jnp.dot(fxt_v[pl.ds(two * 256, 256), :], data, preferred_element_type=F32)
                part = part.reshape(2, 2, 2, KX, HALF)
                real, imag = part[:, 0], part[:, 1]
                turned = jnp.stack([
                    real * cosine + imag * sine,
                    imag * cosine - real * sine,
                ], axis=1).reshape(256, HALF).astype(BF16)
                summed = lax.dot_general(pick, turned, NT, preferred_element_type=F32)
                total[two] = summed if h == 0 else total[two] + summed
        for two in range(2):
            for block in range(2):
                send2[c, two * 2 + block] = total[two][:, block * 128:(block + 1) * 128].astype(BF16)

        for k in (4, 6, 5, 7, 1, 3, 2):
            to, col2, block = near_partner(k)
            pltpu.make_async_remote_copy(
                send2.at[c, block], recv2.at[c, mine2], ssem.at[2 + c], rsem.at[2 + c],
                device_id=(to, col2), device_id_type=MESH,
            ).start()

        recv2[c, mine2] = send2[c, xlo * 2 + core]

    for copy in constants[5:7]:
        copy.wait()

    def turn(mixed, of, c):
        spread = lax.dot_general(mixed, pick, TN, preferred_element_type=F32)
        other = jnp.minimum(of + c, 1)
        cosine, sine = itw_v[other, 0], itw_v[other, 1]
        real, imag = spread[0:64], spread[64:128]
        turned_v[c, of] = jnp.concatenate([
            real * cosine - imag * sine,
            real * sine + imag * cosine,
        ]).astype(BF16)

    for c in range(2):
        wait_bytes(recv2.at[c, pl.ds(0, 7)], rsem.at[2 + c])
        for half in range(2):
            sum4 = recv2[c, half * 4].astype(F32)
            for k in range(1, 4):
                sum4 += recv2[c, half * 4 + k].astype(F32)
            sum4 = sum4.astype(BF16).astype(F32)
            modes[0, pl.ds(half * GROUP, GROUP), :] = sum4
            modes[1, pl.ds(half * GROUP, GROUP), :] = pltpu.roll(sum4, 64, 1)

        def mix(step, mixed):
            rows = pl.ds(pl.multiple_of(step * 8, 8), 8)
            straight, crossed = modes[0, rows, :], modes[1, rows, :]
            for k in range(8):
                i = step * 8 + k
                mixed += wmix[c, 0, i] * straight[k:k + 1] + wmix[c, 1, i] * crossed[k:k + 1]
            return mixed

        own[c] = lax.fori_loop(0, 8, mix, jnp.zeros((GROUP, 128), F32)).astype(BF16)
        pltpu.make_async_remote_copy(
            own.at[c], near.at[c], ssem.at[4 + c], rsem.at[4 + c],
            device_id=(g + 1 - 2 * core, col), device_id_type=MESH,
        ).start()
        turn(own[c], core, c)
    for c in range(2):
        wait_bytes(near.at[c], rsem.at[4 + c])
        turn(near[c], 1 - core, c)

    chip = z * 8 + xlo * 4 + y
    mine3 = (y % 2) * 16 + z * 4 + (y // 2) * 2 + xlo
    for half in range(2):
        tiles = [
            jnp.dot(ixt_v[half], turned_v[c].reshape(256, HALF), preferred_element_type=F32).reshape(32, 8, HALF)
            for c in range(2)
        ]
        send3[half] = jnp.concatenate(tiles, axis=1).astype(BF16)

        def share(k):
            z2, y2 = (z + 2 + 3 * (k // 8)) % 4, (y + 2 + 3 * ((k // 2) % 4)) % 4
            to = z2 * 8 + ((xlo + 1 - k % 2) % 2) * 4 + y2
            pltpu.make_async_remote_copy(
                send3.at[half, to], recv3.at[half, mine3], ssem.at[6 + half], rsem.at[6 + half],
                device_id=(to * 2 + core, col), device_id_type=MESH,
            ).start()

        pl.loop(0, 21)(share)
        pl.loop(22, 32)(share)
        recv3[half, mine3] = send3[half, chip]

    for copy in constants[:2] + constants[7:]:
        copy.wait()
    square = (GROUP, GROUP)
    diagonal = lax.broadcasted_iota(jnp.int32, square, 0) == lax.broadcasted_iota(jnp.int32, square, 1)

    def column(row):
        part = 0.5 * jnp.sum(jnp.where(diagonal, row, 0.0), axis=1, keepdims=True)
        return jnp.broadcast_to(part, (GROUP, PRE))

    gain_c, bias_c = column(gain_v[...]), column(bias_v[...])

    for half, pre in ((0, pre0), (1, pre1)):
        @pl.loop(0, XDEV // 2)
        def _(x):
            start = pl.multiple_of(x * GROUP, GROUP)
            for at in range(0, PLANE, PRE):
                cells = xbuf[pl.ds(start + half * HALF, GROUP), pl.ds(at, PRE)].astype(F32)
                pre[pl.ds(start, GROUP), pl.ds(at, PRE)] = cells * gain_c + bias_c

    for c in range(2):
        wait_bytes(send1.at[c, pl.ds(0, 30)], ssem.at[c])
        wait_bytes(recv2.at[c, pl.ds(0, 7)], ssem.at[2 + c])
        wait_bytes(own.at[c], ssem.at[4 + c])

    def put(n, s, rows, values):
        out[rows, pl.ds(s * FOLD + n * BLOCK, BLOCK)] = values

    wait_bytes(recv3.at[0, pl.ds(0, 31)], rsem.at[6])
    arrange(recv3[0], vals)
    transform_back(vals, pre0, tbuf, evens, odds, put, lambda n: None)
    wait_bytes(recv3.at[1, pl.ds(0, 31)], rsem.at[7])
    shares[...] = recv3[1]
    for half in range(2):
        wait_bytes(send3.at[half, pl.ds(0, 31)], ssem.at[6 + half])


def finish_kernel(first, shares, pre, table, out, vals, obuf, evens, odds, fsem, osem):
    per = STEP // BLOCK

    def store(j, s):
        cols = pl.ds(s * FOLD + j * STEP, STEP)
        return pltpu.make_async_copy(obuf.at[:, cols], out.at[pl.ds(HALF, HALF), cols], osem.at[j, s])

    def put(n, s, rows, values):
        obuf[rows, pl.ds(s * FOLD + n * BLOCK, BLOCK)] = values

    def after(n):
        if n % per == per - 1:
            store(n // per, 0).start()
            store(n // per, 1).start()

    first_half = pltpu.make_async_copy(first, out.at[pl.ds(0, HALF), :], fsem)
    first_half.start()
    arrange(shares[...], vals)
    transform_back(vals, pre, table, evens, odds, put, after)
    for j in range(FOLD // STEP):
        store(j, 0).wait()
        store(j, 1).wait()
    first_half.wait()


def in_hbm(array):
    return pltpu.with_memory_space_constraint(array, pltpu.HBM)


def shards(state_field, spectral_weight, local_weight, channel_bias):
    anywhere = pl.BlockSpec(memory_space=pltpu.HBM)
    vmem = pl.BlockSpec(memory_space=pltpu.VMEM)
    first, shares, pre, table_v = pl.pallas_call(
        exchange_kernel,
        out_shape=[
            jax.ShapeDtypeStruct((HALF, PLANE), BF16),
            jax.ShapeDtypeStruct((32, 16, HALF), BF16),
            jax.ShapeDtypeStruct((HALF, PLANE), F32),
            jax.ShapeDtypeStruct((512, FOLD), BF16),
        ],
        in_specs=[anywhere] * 9,
        out_specs=[vmem] * 4,
        scratch_shapes=[
            pltpu.VMEM((ROWS, PLANE), BF16),
            pltpu.VMEM((2, 64, GROUP, 128), BF16),
            pltpu.VMEM((1, GROUP), F32),
            pltpu.VMEM((1, GROUP), F32),
            pltpu.VMEM((512, 256), BF16),
            pltpu.VMEM((2, KX, ROWS), F32),
            pltpu.VMEM((2, 256, 256), BF16),
            pltpu.VMEM((2, 2, 64, HALF), F32),
            pltpu.VMEM((2, 2, 64, GROUP, 128), F32),
            pltpu.VMEM((2, 32, 16, HALF), BF16),
            pltpu.VMEM((2, 32, 16, HALF), BF16),
            pltpu.VMEM((2, 4, GROUP, 128), BF16),
            pltpu.VMEM((2, 8, GROUP, 128), BF16),
            pltpu.VMEM((2, 64, 128), F32),
            pltpu.VMEM((2, GROUP, 128), BF16),
            pltpu.VMEM((2, GROUP, 128), BF16),
            pltpu.VMEM((2, 2, 128, HALF), BF16),
            pltpu.VMEM((2, 32, 16, HALF), BF16),
            pltpu.VMEM((2, 32, 16, HALF), BF16),
            pltpu.VMEM((HALF, PLANE), F32),
            pltpu.VMEM((HALF, 512), BF16),
            pltpu.VMEM((2, HALF, BLOCK), F32),
            pltpu.VMEM((2, HALF, BLOCK), F32),
            pltpu.SemaphoreType.DMA((3,)),
            pltpu.SemaphoreType.DMA((4 * PIECES,)),
            pltpu.SemaphoreType.DMA((7,)),
            pltpu.SemaphoreType.DMA((8,)),
            pltpu.SemaphoreType.DMA((8,)),
        ],
        compiler_params=pltpu.CompilerParams(
            collective_id=0, has_side_effects=True, vmem_limit_bytes=32 << 20
        ),
        name="exchange",
    )(
        in_hbm(state_field.reshape(ROWS, PLANE)),
        in_hbm(spectral_weight),
        in_hbm(local_weight.reshape(1, GROUP)),
        in_hbm(channel_bias.reshape(1, GROUP)),
        *[in_hbm(jnp.asarray(make())) for make in (
            plane_table, forward_x_table, forward_twiddle, inverse_x_table, inverse_twiddle
        )],
    )
    result = pl.pallas_call(
        finish_kernel,
        out_shape=jax.ShapeDtypeStruct((ROWS, PLANE), BF16),
        in_specs=[vmem] * 4,
        out_specs=anywhere,
        scratch_shapes=[
            pltpu.VMEM((HALF, 512), BF16),
            pltpu.VMEM((HALF, PLANE), BF16),
            pltpu.VMEM((2, HALF, BLOCK), F32),
            pltpu.VMEM((2, HALF, BLOCK), F32),
            pltpu.SemaphoreType.DMA,
            pltpu.SemaphoreType.DMA((FOLD // STEP, 2)),
        ],
        compiler_params=pltpu.CompilerParams(vmem_limit_bytes=16 << 20),
        name="finish",
    )(first, shares, pre, table_v)
    return result.reshape(state_field.shape)


def solution(mesh):
    return jax.shard_map(
        shards,
        mesh=mesh,
        in_specs=(P("gx", "col", None), P(None, None, "col", "gx"), P("col"), P("col")),
        out_specs=P("gx", "col", None),
        check_vma=False,
    )
```

```python
import math

import jax
import jax.numpy as jnp
import ml_dtypes
import numpy as np
from jax import lax
from jax.experimental import pallas as pl
from jax.experimental.pallas import tpu as pltpu
from jax.sharding import PartitionSpec as P

MESH = pl.DeviceIdType.MESH
BF16 = jnp.bfloat16
F32 = jnp.float32

XCELLS = 1024
YCELLS = 128
TSTEPS = 64
KX = 32
KY = 32
PLANE = YCELLS * TSTEPS
FOLD = PLANE // 2
QUARTER = PLANE // 4
XDEV = 16
GROUP = 32
ROWS = XDEV * GROUP
HALF = ROWS // 2
PIECES = 4
PIECE = FOLD // PIECES
STEP = 512
BLOCK = 256
MB = 64
PRE = 256

NT = (((1,), (1,)), ((), ()))
TN = (((0,), (0,)), ((), ()))


FAR_FIRST = sorted(
    [(dz, dy) for dz in range(4) for dy in range(4) if dz or dy],
    key=lambda o: -(min(o[0], 4 - o[0]) + min(o[1], 4 - o[1])),
)


def freq(index, number):
    return np.where(index < number // 2, index, index - number)


def plane_table():
    p, z, yh, c, xlo, half, r, kt2 = np.meshgrid(
        *[np.arange(n) for n in (2, 4, 2, 2, 2, 2, 2, 2)], indexing="ij"
    )
    ky = freq((z * 8 + xlo * 4 + yh * 2 + p).reshape(-1), KY)
    kt = (half * 4 + c * 2 + kt2).reshape(-1)
    r = r.reshape(-1)
    cells = np.arange(FOLD)
    y, t = cells // TSTEPS, cells % TSTEPS
    phase = (ky[:, None] * y[None] * TSTEPS + kt[:, None] * t[None] * YCELLS) % PLANE
    angle = phase * (2.0 * math.pi / PLANE)
    table = np.where(r[:, None] == 0, np.cos(angle), -np.sin(angle))
    return table.astype(ml_dtypes.bfloat16)


def forward_x_table():
    kx = freq(np.arange(KX), KX)
    slot = np.arange(16)
    p, z, yh = slot // 8, (slot // 2) % 4, slot % 2
    angle = 2.0 * math.pi * ((kx[:, None] * (8 * z + yh * 2 + p)[None]) % 32) / 32
    cosine, sine = np.cos(angle), np.sin(angle)
    table = np.zeros((4, 2, 2, KX, 16, 4, 2, 2))
    for block in range(4):
        for k in range(2):
            table[block, 0, k, :, :, block, 0, k] = cosine
            table[block, 0, k, :, :, block, 1, k] = sine
            table[block, 1, k, :, :, block, 1, k] = cosine
            table[block, 1, k, :, :, block, 0, k] = -sine
    return table.reshape(512, 256).astype(ml_dtypes.bfloat16)


def forward_twiddle():
    kx = freq(np.arange(KX), KX)
    scale = 1.0 / math.sqrt(XCELLS * PLANE)
    place = np.arange(4)
    offset = (place // 2) * 128 + (place % 2) * 16
    lanes = np.arange(ROWS) // GROUP
    angle = 2.0 * math.pi * ((kx[None, :, None] * (offset[:, None, None] + lanes)) % XCELLS) / XCELLS
    return (np.stack([np.cos(angle), np.sin(angle)], axis=1) * scale).astype(np.float32)


def inverse_x_table():
    kx = freq(np.arange(KX), KX)
    start = np.arange(2)[:, None] * 8 + np.arange(32)[None] * 32
    angle = 2.0 * math.pi * ((kx * start[..., None]) % XCELLS) / XCELLS
    cosine, sine = np.cos(angle), np.sin(angle)
    table = np.zeros((2, 32, 2, 2, 2, 2, 2, 2, KX))
    for core in range(2):
        for k in range(2):
            table[:, :, core, 0, k, core, 0, k] = cosine
            table[:, :, core, 0, k, core, 1, k] = -sine
            table[:, :, core, 1, k, core, 0, k] = sine
            table[:, :, core, 1, k, core, 1, k] = cosine
    return table.reshape(2, 256, 256).astype(ml_dtypes.bfloat16)


def inverse_twiddle():
    kx = np.tile(freq(np.arange(KX), KX), 2)
    kt2 = np.repeat(np.arange(2), KX)
    lanes = np.arange(2)[:, None] * XDEV + np.arange(HALF)[None] // GROUP
    angle = 2.0 * math.pi * ((kx[None, :, None] * lanes[:, None]) % XCELLS) / XCELLS
    parts = np.stack([np.cos(angle), np.sin(angle)], axis=1)
    weight = np.stack([np.where(kt2 + 2 * other == 0, 1.0, 2.0) for other in range(2)])
    scale = 0.5 / math.sqrt(PLANE)
    return (parts[:, None] * weight[None, :, None, :, None] * scale).astype(np.float32)


def place_of(g):
    return g // 16, (g // 8) % 2, (g // 2) % 4, g % 2


def arrange(shares, vals):
    tiles = shares.astype(F32).reshape(16, 2, 2, 8, HALF)
    tiles = jnp.stack([tiles[:, 0, 0], tiles[:, 1, 0], tiles[:, 0, 1], tiles[:, 1, 1]], axis=1)
    vals[...] = tiles.reshape(512, HALF).T.astype(BF16)


def transform_back(vals, pre, table, evens, odds, put, after):
    c1 = 2.0 * math.sqrt(2.0 / math.pi)
    c3 = 8.0 * 0.044715 * math.sqrt(2.0 / math.pi)

    def products(n):
        cols = pl.ds(n * BLOCK, BLOCK)
        evens[n % 2] = jnp.dot(vals[:, 0:256], table[0:256, cols], preferred_element_type=F32)
        odds[n % 2] = jnp.dot(vals[:, 256:512], table[256:512, cols], preferred_element_type=F32)

    products(0)
    for n in range(FOLD // BLOCK):
        if (n + 1) * BLOCK < FOLD:
            products(n + 1)
        for m in range(HALF // MB):
            rows = pl.ds(m * MB, MB)
            even, odd = evens[n % 2, rows, :], odds[n % 2, rows, :]
            for s in range(2):
                spectral = even + odd if s == 0 else even - odd
                v = spectral + pre[rows, pl.ds(s * FOLD + n * BLOCK, BLOCK)]
                u = v * (c1 + c3 * (v * v))
                put(n, s, rows, (v + v * jnp.tanh(u)).astype(BF16))
        after(n)


def exchange_kernel(
    state, weight, gain, bias, table, fxt, ftw, ixt, itw, out, shares, pre1, tbuf,
    xbuf, wbuf, gain_v, bias_v, fxt_v, ftw_v, ixt_v, itw_v, wmix,
    send1, recv1, send2, recv2, modes, own, near, turned_v, send3, recv3,
    pre0, vals, evens, odds,
    tsem, xsem, csem, ssem, rsem,
):
    g = lax.axis_index("gx")
    col = lax.axis_index("col")
    z, xlo, y, core = place_of(g)

    def zy_partner(dz, dy):
        z2, y2 = (z + dz) % 4, (y + dy) % 4
        return z2 * 16 + xlo * 8 + y2 * 2 + core, (y2 % 2) * 8 + z2 * 2 + y2 // 2

    def near_partner(k):
        xlo2, core2, col2 = (xlo + k % 2) % 2, (core + (k // 2) % 2) % 2, (col + k // 4) % 2
        return z * 16 + xlo2 * 8 + y * 2 + core2, col2, xlo2 * 2 + core2

    def wait_bytes(ref, sem):
        pltpu.make_async_copy(ref, ref, sem).wait()

    table_loads = []
    for k in range(2):
        cols = pl.ds(k * PIECE, PIECE)
        table_loads.append(pltpu.make_async_copy(table.at[:, cols], tbuf.at[:, cols], tsem.at[k]))
    rest = pl.ds(QUARTER, QUARTER)
    table_loads.append(pltpu.make_async_copy(table.at[:, rest], tbuf.at[:, rest], tsem.at[2]))
    state_loads = {}
    for h in range(2):
        for k in range(PIECES):
            for s in range(2):
                rows, at = pl.ds(h * HALF, HALF), pl.ds(s * FOLD + k * PIECE, PIECE)
                state_loads[h, k, s] = pltpu.make_async_copy(
                    state.at[rows, at], xbuf.at[rows, at], xsem.at[(h * PIECES + k) * 2 + s]
                )
    for k in range(PIECES):
        if k < 2:
            table_loads[k].start()
        for s in range(2):
            state_loads[0, k, s].start()
    constants = [
        pltpu.make_async_copy(gain, gain_v, csem.at[0]),
        pltpu.make_async_copy(bias, bias_v, csem.at[1]),
        pltpu.make_async_copy(weight, wbuf, csem.at[2]),
        pltpu.make_async_copy(fxt, fxt_v, csem.at[3]),
        pltpu.make_async_copy(ftw.at[xlo * 2 + core], ftw_v, csem.at[4]),
        pltpu.make_async_copy(itw.at[core], itw_v, csem.at[5]),
        pltpu.make_async_copy(ixt, ixt_v, csem.at[6]),
        table_loads[2],
    ]

    barrier = pltpu.get_barrier_semaphore()

    @pl.loop(1, 32)
    def _(k):
        to = (g + 2 * k) % 64
        pl.semaphore_signal(barrier, inc=1, device_id=(to, col), device_id_type=MESH)

    @pl.loop(2, 8)
    def _(k):
        to, col2, _slot = near_partner(k)
        pl.semaphore_signal(barrier, inc=1, device_id=(to, col2), device_id_type=MESH)

    row4 = lax.broadcasted_iota(jnp.int32, (256, HALF), 0) % 4
    mine1 = (y % 2) * 8 + z * 2 + y // 2
    for h in range(2):
        rows = pl.ds(h * HALF, HALF)
        sums = [[None, None], [None, None]]
        for k in range(PIECES):
            lo = pl.ds(k * PIECE, PIECE)
            hi = pl.ds(FOLD + k * PIECE, PIECE)
            cols = pl.ds((k % 2) * PIECE, PIECE)
            if h == 0 and k < 2:
                table_loads[k].wait()
            for s in range(2):
                state_loads[h, k, s].wait()
                if h == 0:
                    state_loads[1, k, s].start()
            x0, x1 = xbuf[rows, lo], xbuf[rows, hi]
            for p, x in ((0, x0 + x1), (1, x0 - x1)):
                part = lax.dot_general(
                    tbuf[pl.ds(p * 256, 256), cols], x, NT, preferred_element_type=F32
                )
                before = sums[p][k // 2]
                sums[p][k // 2] = part if before is None else before + part
        swapped = jnp.where(row4 < 2, pltpu.roll(sums[1][1], 254, 0), -pltpu.roll(sums[1][1], 2, 0))
        for p, second in ((0, sums[0][1]), (1, swapped)):
            first = sums[p][0].reshape(4, 2, 32, HALF)
            second = second.reshape(4, 2, 32, HALF)
            even, odd = first[:, 0] + second[:, 0], first[:, 1] - second[:, 1]
            both = jnp.stack([even, odd], axis=1).astype(BF16).reshape(8, 2, 16, HALF)
            for c in range(2):
                send1[c, pl.ds(h * 16 + p * 8, 8)] = both[:, c]
        if h == 0:
            for copy in constants:
                copy.start()
            pl.semaphore_wait(barrier, 37)
        for c in range(2):
            for dz, dy in FAR_FIRST:
                to, slot = zy_partner(dz, dy)
                pltpu.make_async_remote_copy(
                    send1.at[c, h * 16 + slot], recv1.at[c, h * 16 + mine1], ssem.at[c], rsem.at[c],
                    device_id=(to, col), device_id_type=MESH,
                ).start()

            recv1[c, h * 16 + mine1] = send1[c, h * 16 + mine1]

    constants[2].wait()
    left = lax.broadcasted_iota(jnp.int32, (GROUP, 128), 1) < 64

    @pl.loop(0, 64)
    def _(i):
        wr, wi = wbuf[0, i].astype(F32), wbuf[1, i].astype(F32)
        wr2, wi2 = pltpu.roll(wr, 64, 1), pltpu.roll(wi, 64, 1)
        wmix[0, 0, i] = jnp.where(left, wr, wr2)
        wmix[0, 1, i] = jnp.where(left, -wi, wi2)
        wmix[1, 0, i] = jnp.where(left, wr2, wr)
        wmix[1, 1, i] = jnp.where(left, -wi2, wi)

    for copy in constants[3:5]:
        copy.wait()
    lane_c = lax.broadcasted_iota(jnp.int32, (GROUP, HALF), 1) % GROUP
    row_c = lax.broadcasted_iota(jnp.int32, (GROUP, HALF), 0)
    pick = jnp.where(lane_c == row_c, 1.0, 0.0).astype(BF16)

    mine2 = col * 4 + xlo * 2 + core
    for c in range(2):
        wait_bytes(recv1.at[c, pl.ds(0, 30)], rsem.at[c])
        total = [None] * 2
        for h in range(2):
            lanes = pl.ds(h * HALF, HALF)
            data = recv1[c, pl.ds(h * 16, 16)].reshape(256, HALF)
            cosine, sine = ftw_v[0, :, lanes], ftw_v[1, :, lanes]
            for two in range(2):
                part = jnp.dot(fxt_v[pl.ds(two * 256, 256), :], data, preferred_element_type=F32)
                part = part.reshape(2, 2, 2, KX, HALF)
                real, imag = part[:, 0], part[:, 1]
                turned = jnp.stack([
                    real * cosine + imag * sine,
                    imag * cosine - real * sine,
                ], axis=1).reshape(256, HALF).astype(BF16)
                summed = lax.dot_general(pick, turned, NT, preferred_element_type=F32)
                total[two] = summed if h == 0 else total[two] + summed
        for two in range(2):
            for block in range(2):
                send2[c, two * 2 + block] = total[two][:, block * 128:(block + 1) * 128].astype(BF16)

        for k in (4, 6, 5, 7, 1, 3, 2):
            to, col2, block = near_partner(k)
            pltpu.make_async_remote_copy(
                send2.at[c, block], recv2.at[c, mine2], ssem.at[2 + c], rsem.at[2 + c],
                device_id=(to, col2), device_id_type=MESH,
            ).start()

        recv2[c, mine2] = send2[c, xlo * 2 + core]

    for copy in constants[5:7]:
        copy.wait()

    def turn(mixed, of, c):
        spread = lax.dot_general(mixed, pick, TN, preferred_element_type=F32)
        other = jnp.minimum(of + c, 1)
        cosine, sine = itw_v[other, 0], itw_v[other, 1]
        real, imag = spread[0:64], spread[64:128]
        turned_v[c, of] = jnp.concatenate([
            real * cosine - imag * sine,
            real * sine + imag * cosine,
        ]).astype(BF16)

    for c in range(2):
        wait_bytes(recv2.at[c, pl.ds(0, 7)], rsem.at[2 + c])
        for half in range(2):
            sum4 = recv2[c, half * 4].astype(F32)
            for k in range(1, 4):
                sum4 += recv2[c, half * 4 + k].astype(F32)
            sum4 = sum4.astype(BF16).astype(F32)
            modes[0, pl.ds(half * GROUP, GROUP), :] = sum4
            modes[1, pl.ds(half * GROUP, GROUP), :] = pltpu.roll(sum4, 64, 1)

        def mix(step, mixed):
            rows = pl.ds(pl.multiple_of(step * 8, 8), 8)
            straight, crossed = modes[0, rows, :], modes[1, rows, :]
            for k in range(8):
                i = step * 8 + k
                mixed += wmix[c, 0, i] * straight[k:k + 1] + wmix[c, 1, i] * crossed[k:k + 1]
            return mixed

        own[c] = lax.fori_loop(0, 8, mix, jnp.zeros((GROUP, 128), F32)).astype(BF16)
        pltpu.make_async_remote_copy(
            own.at[c], near.at[c], ssem.at[4 + c], rsem.at[4 + c],
            device_id=(g + 1 - 2 * core, col), device_id_type=MESH,
        ).start()
        turn(own[c], core, c)
    for c in range(2):
        wait_bytes(near.at[c], rsem.at[4 + c])
        turn(near[c], 1 - core, c)

    chip = z * 8 + xlo * 4 + y
    mine3 = (y % 2) * 16 + z * 4 + (y // 2) * 2 + xlo
    for half in range(2):
        tiles = [
            jnp.dot(ixt_v[half], turned_v[c].reshape(256, HALF), preferred_element_type=F32).reshape(32, 8, HALF)
            for c in range(2)
        ]
        send3[half] = jnp.concatenate(tiles, axis=1).astype(BF16)

        def share(k):
            z2, y2 = (z + 2 + 3 * (k // 8)) % 4, (y + 2 + 3 * ((k // 2) % 4)) % 4
            to = z2 * 8 + ((xlo + 1 - k % 2) % 2) * 4 + y2
            pltpu.make_async_remote_copy(
                send3.at[half, to], recv3.at[half, mine3], ssem.at[6 + half], rsem.at[6 + half],
                device_id=(to * 2 + core, col), device_id_type=MESH,
            ).start()

        pl.loop(0, 21)(share)
        pl.loop(22, 32)(share)
        recv3[half, mine3] = send3[half, chip]

    for copy in constants[:2] + constants[7:]:
        copy.wait()
    square = (GROUP, GROUP)
    diagonal = lax.broadcasted_iota(jnp.int32, square, 0) == lax.broadcasted_iota(jnp.int32, square, 1)

    def column(row):
        part = 0.5 * jnp.sum(jnp.where(diagonal, row, 0.0), axis=1, keepdims=True)
        return jnp.broadcast_to(part, (GROUP, PRE))

    gain_c, bias_c = column(gain_v[...]), column(bias_v[...])

    for half, pre in ((0, pre0), (1, pre1)):
        @pl.loop(0, XDEV // 2)
        def _(x):
            start = pl.multiple_of(x * GROUP, GROUP)
            for at in range(0, PLANE, PRE):
                cells = xbuf[pl.ds(start + half * HALF, GROUP), pl.ds(at, PRE)].astype(F32)
                pre[pl.ds(start, GROUP), pl.ds(at, PRE)] = cells * gain_c + bias_c

    for c in range(2):
        wait_bytes(send1.at[c, pl.ds(0, 30)], ssem.at[c])
        wait_bytes(recv2.at[c, pl.ds(0, 7)], ssem.at[2 + c])
        wait_bytes(own.at[c], ssem.at[4 + c])

    def put(n, s, rows, values):
        out[rows, pl.ds(s * FOLD + n * BLOCK, BLOCK)] = values

    wait_bytes(recv3.at[0, pl.ds(0, 31)], rsem.at[6])
    arrange(recv3[0], vals)
    transform_back(vals, pre0, tbuf, evens, odds, put, lambda n: None)
    wait_bytes(recv3.at[1, pl.ds(0, 31)], rsem.at[7])
    shares[...] = recv3[1]
    for half in range(2):
        wait_bytes(send3.at[half, pl.ds(0, 31)], ssem.at[6 + half])


def finish_kernel(first, shares, pre, table, out, vals, obuf, evens, odds, fsem, osem):
    per = STEP // BLOCK

    def store(j, s):
        cols = pl.ds(s * FOLD + j * STEP, STEP)
        return pltpu.make_async_copy(obuf.at[:, cols], out.at[pl.ds(HALF, HALF), cols], osem.at[j, s])

    def put(n, s, rows, values):
        obuf[rows, pl.ds(s * FOLD + n * BLOCK, BLOCK)] = values

    def after(n):
        if n % per == per - 1:
            store(n // per, 0).start()
            store(n // per, 1).start()

    first_half = []
    for k in range(4):
        rows = pl.ds(k * MB, MB)
        first_half.append(pltpu.make_async_copy(first.at[rows, :], out.at[rows, :], fsem.at[k]))
        first_half[-1].start()
    arrange(shares[...], vals)
    transform_back(vals, pre, table, evens, odds, put, after)
    for j in range(FOLD // STEP):
        store(j, 0).wait()
        store(j, 1).wait()
    for copy in first_half:
        copy.wait()


def in_hbm(array):
    return pltpu.with_memory_space_constraint(array, pltpu.HBM)


def shards(state_field, spectral_weight, local_weight, channel_bias):
    anywhere = pl.BlockSpec(memory_space=pltpu.HBM)
    vmem = pl.BlockSpec(memory_space=pltpu.VMEM)
    first, shares, pre, table_v = pl.pallas_call(
        exchange_kernel,
        out_shape=[
            jax.ShapeDtypeStruct((HALF, PLANE), BF16),
            jax.ShapeDtypeStruct((32, 16, HALF), BF16),
            jax.ShapeDtypeStruct((HALF, PLANE), F32),
            jax.ShapeDtypeStruct((512, FOLD), BF16),
        ],
        in_specs=[anywhere] * 9,
        out_specs=[vmem] * 4,
        scratch_shapes=[
            pltpu.VMEM((ROWS, PLANE), BF16),
            pltpu.VMEM((2, 64, GROUP, 128), BF16),
            pltpu.VMEM((1, GROUP), F32),
            pltpu.VMEM((1, GROUP), F32),
            pltpu.VMEM((512, 256), BF16),
            pltpu.VMEM((2, KX, ROWS), F32),
            pltpu.VMEM((2, 256, 256), BF16),
            pltpu.VMEM((2, 2, 64, HALF), F32),
            pltpu.VMEM((2, 2, 64, GROUP, 128), F32),
            pltpu.VMEM((2, 32, 16, HALF), BF16),
            pltpu.VMEM((2, 32, 16, HALF), BF16),
            pltpu.VMEM((2, 4, GROUP, 128), BF16),
            pltpu.VMEM((2, 8, GROUP, 128), BF16),
            pltpu.VMEM((2, 64, 128), F32),
            pltpu.VMEM((2, GROUP, 128), BF16),
            pltpu.VMEM((2, GROUP, 128), BF16),
            pltpu.VMEM((2, 2, 128, HALF), BF16),
            pltpu.VMEM((2, 32, 16, HALF), BF16),
            pltpu.VMEM((2, 32, 16, HALF), BF16),
            pltpu.VMEM((HALF, PLANE), F32),
            pltpu.VMEM((HALF, 512), BF16),
            pltpu.VMEM((2, HALF, BLOCK), F32),
            pltpu.VMEM((2, HALF, BLOCK), F32),
            pltpu.SemaphoreType.DMA((3,)),
            pltpu.SemaphoreType.DMA((4 * PIECES,)),
            pltpu.SemaphoreType.DMA((7,)),
            pltpu.SemaphoreType.DMA((8,)),
            pltpu.SemaphoreType.DMA((8,)),
        ],
        compiler_params=pltpu.CompilerParams(
            collective_id=0, has_side_effects=True, vmem_limit_bytes=32 << 20
        ),
        name="exchange",
    )(
        in_hbm(state_field.reshape(ROWS, PLANE)),
        in_hbm(spectral_weight),
        in_hbm(local_weight.reshape(1, GROUP)),
        in_hbm(channel_bias.reshape(1, GROUP)),
        *[in_hbm(jnp.asarray(make())) for make in (
            plane_table, forward_x_table, forward_twiddle, inverse_x_table, inverse_twiddle
        )],
    )
    result = pl.pallas_call(
        finish_kernel,
        out_shape=jax.ShapeDtypeStruct((ROWS, PLANE), BF16),
        in_specs=[vmem] * 4,
        out_specs=anywhere,
        scratch_shapes=[
            pltpu.VMEM((HALF, 512), BF16),
            pltpu.VMEM((HALF, PLANE), BF16),
            pltpu.VMEM((2, HALF, BLOCK), F32),
            pltpu.VMEM((2, HALF, BLOCK), F32),
            pltpu.SemaphoreType.DMA((4,)),
            pltpu.SemaphoreType.DMA((FOLD // STEP, 2)),
        ],
        compiler_params=pltpu.CompilerParams(vmem_limit_bytes=16 << 20),
        name="finish",
    )(first, shares, pre, table_v)
    return result.reshape(state_field.shape)


def solution(mesh):
    return jax.shard_map(
        shards,
        mesh=mesh,
        in_specs=(P("gx", "col", None), P(None, None, "col", "gx"), P("col"), P("col")),
        out_specs=P("gx", "col", None),
        check_vma=False,
    )
```
